256 devices in a mesh: dp: 32 (over x, z_lo, core), inner: 2 (over z_hi), outer: 4 (over y).
Axes of the slice: x: 4, y: 4, z: 8 (z_hi: 2, z_lo: 4; z = z_hi * 4 + z_lo), core: 2. Of those that a mesh axis runs over, the one named last changes fastest.
Arguments:
- partials: bfloat16 [256, 120, 16384], P(('dp', 'inner', 'outer')), parts along dimension 0, may hold values from -5 to 5
- residual: bfloat16 [3840, 16384], P('dp', ('inner', 'outer')), parts along dimension 0, may hold values from -18 to 18
- norm_gain: float32 [16384], replicated, may hold values from 0.25 to 1.75
- kv_weight: bfloat16 [16384, 8, 256], P(None, ('inner', 'outer')), may hold values from -0.046875 to 0.046875
Outputs:
- stream: bfloat16 [3840, 16384], P('dp', ('inner', 'outer')), parts along dimension 0
- kv_pair: bfloat16 [3840, 8, 256], P('dp', ('inner', 'outer')), parts along dimension 0
The draws below stay inside these ranges and needn't reach their ends.
There are 32 independent parts, one for each index of `dp`. The reference program is written for one: setup_inputs(seed, part) draws one part's arguments, and reference() takes and returns one part's arrays. A program takes and returns all parts, laid end to end along the dimension named above; an argument that names none is the same for every part. Nothing has to cross between parts.
All inputs are finite; a program needn't handle non-finite values.
Results may differ from the reference program's by a relative error of at most 0.015.
Values may be sent and summed in bfloat16 or wider, within the bound.
No kernel may reach another device: no remote copies, remote signals or barrier semaphores. Data moves between devices by JAX's collectives and lax.ppermute only.
A program may use at most 128 MiB of HBM per device.

```python
import jax
import jax.numpy as jnp
from jax import lax

D = 16384
KV_HEADS = 8
HEAD = 128
SPAN = 120
TP = 8
N_INNER = 2
N_OUTER = 4


def draw_residual(key, part):
    key = jax.random.fold_in(key, 7)
    column = jnp.arange(D, dtype=jnp.float32) / (D - 1)
    spread = 0.3 * jnp.power(10.0, column)
    base = jnp.clip(jax.random.normal(key, (SPAN, D), jnp.float32), -6.0, 6.0)
    return (base * spread[None, :]).astype(jnp.bfloat16)


def with_spikes(values, stream_key, source, target, blocks, factor):
    owner, partner = [(jnp.arange(values.shape[axis_at]) // (values.shape[axis_at] // blocks)).reshape([-1 if axis == axis_at else 1 for axis in range(values.ndim)]) for axis_at in (source, target)]
    chosen = jax.random.permutation(stream_key, blocks)[partner]
    strong = (owner == chosen) | (owner == (partner + blocks // 2) % blocks)
    return jnp.where(strong, factor * values, values)


def shard_levels(key, extent, split, low, high):
    level = 1.0
    for position, shards_of in split:
        steps = jax.random.uniform(jax.random.fold_in(jax.random.fold_in(key, 6), position), (shards_of,), jnp.float32, low / len(split), high / len(split))
        level = level * jnp.repeat(jnp.exp(steps), extent[position] // shards_of).reshape((-1,) + (1,) * (len(extent) - 1 - position))
    return level


def normal_values(rng, dims, scale, bound, pieces=(), kind=jnp.bfloat16):
    level = shard_levels(rng, dims, pieces, -0.22, 0.18) if pieces else 1.0
    drawn = jax.random.normal(rng, dims, jnp.float32) * scale * level
    return jnp.minimum(jnp.maximum(drawn, -bound), bound).astype(kind)


def noise_with(key, dims, scale, most, split, heavy, kind=jnp.bfloat16):
    values = scale * jax.random.normal(key, dims, jnp.float32)
    if split:
        values = values * shard_levels(key, dims, split, -0.22, 0.18)
    return jnp.clip(with_spikes(values, jax.random.fold_in(key, 3), *heavy), -most, most).astype(kind)


def setup_inputs(seed: int = 0, part: int = 0) -> dict:
    key_of = jax.random.split(jax.random.key(seed), 5)
    part_keys = jax.random.split(jax.random.fold_in(key_of[4], part), 5)
    partials = noise_with(part_keys[0], (TP, SPAN, D), 0.25, 5.0, ((0, 8),), (0, 2, 8, 2.0))
    residual = draw_residual(jax.random.fold_in(jax.random.fold_in(key_of[4], part), 71), part)
    norm_gain = jnp.clip(1.0 + 0.15 * jax.random.normal(key_of[2], (D,), jnp.float32), 0.25, 1.75)
    kv_weight = normal_values(key_of[3], (D, KV_HEADS, 2 * HEAD), D ** -0.5, 0.046875, ((1, 8),))
    return dict(partials=partials, residual=residual, norm_gain=norm_gain, kv_weight=kv_weight)


def reference(partials, residual, norm_gain, kv_weight):
    grouped = partials.astype(jnp.float32).reshape(N_INNER, N_OUTER, SPAN, D)
    level_one = lax.optimization_barrier(jnp.sum(grouped, axis=0)).astype(jnp.bfloat16)
    level_one = lax.optimization_barrier(level_one).astype(jnp.float32)
    level_two = lax.optimization_barrier(jnp.sum(level_one, axis=0))
    stream = (residual.astype(jnp.float32) + level_two).astype(jnp.bfloat16)
    values = stream.astype(jnp.float32)
    factor = lax.rsqrt(lax.optimization_barrier(jnp.mean(values * values, axis=1)) + 1e-05)
    normed = (values * factor[:, None] * norm_gain[None, :]).astype(jnp.bfloat16)
    flat = kv_weight.reshape(D, KV_HEADS * 2 * HEAD)
    kv_pair = jnp.dot(normed, flat, preferred_element_type=jnp.float32).astype(jnp.bfloat16)
    return (stream, kv_pair.reshape(SPAN, KV_HEADS, 2 * HEAD))
```

```python
import functools

import jax
import jax.numpy as jnp
from jax import lax
from jax.experimental import pallas as pl
from jax.experimental.pallas import tpu as pltpu
from jax.sharding import Mesh
from jax.sharding import PartitionSpec as P

BF = jnp.bfloat16
F32 = jnp.float32
OUTER = 4
UNIT = 256
CHUNKS = (256, 512, 640, 640)
VMEM = pl.BlockSpec(memory_space=pltpu.VMEM)
ANY = pl.BlockSpec(memory_space=pl.ANY)
SMEM = pl.BlockSpec(memory_space=pltpu.SMEM)
PAIR_A = [(o, o ^ 1) for o in range(4)]
PAIR_B = [(o, o ^ 3) for o in range(4)]
SWAP = [(0, 1), (1, 0)]


def shift(k):
    return [(o, (o + k) % 4) for o in range(4)]


def params(**more):
    return pltpu.CompilerParams(vmem_limit_bytes=48 * 1024 * 1024, **more)


def cost(flops, nbytes):
    return pl.CostEstimate(flops=flops, bytes_accessed=nbytes, transcendentals=0)


def pick_columns(partial, block_ids, n, start, n_out):
    rows, width = partial.shape
    block = width // 8
    per, first = block // 128, start // 128
    unit = 128

    def spec(t):
        return pl.BlockSpec(
            (rows, unit), lambda g, ids: (0, ids[t] * per + first + g)
        )

    def kernel(ids, *refs):
        ins, outs = refs[: 2 * n_out], refs[2 * n_out :]
        for j in range(n_out):
            outs[j][0] = ins[2 * j][...]
            outs[j][1] = ins[2 * j + 1][...]

    return pl.pallas_call(
        kernel,
        grid_spec=pltpu.PrefetchScalarGridSpec(
            num_scalar_prefetch=1,
            grid=(n // unit,),
            in_specs=[spec(t) for t in range(2 * n_out)],
            out_specs=[
                pl.BlockSpec((2, rows, unit), lambda g, ids: (0, 0, g))
                for _ in range(n_out)
            ],
        ),
        out_shape=[jax.ShapeDtypeStruct((2, rows, n), BF)] * n_out,
        compiler_params=params(),
        cost_estimate=cost(0, 8 * n_out * rows * n),
    )(block_ids, *([partial] * (2 * n_out)))


def first_add(partial, block_ids, from_a, from_b, start):
    rows, width = partial.shape
    n = from_a.shape[2]
    per, first = width // 8 // 128, start // 128
    unit = 128

    def spec(t):
        return pl.BlockSpec(
            (rows, unit), lambda g, ids: (0, ids[t] * per + first + g)
        )

    def kernel(ids, a0, a1, b0, b1, ra, rb, to_a, to_b, keep):
        keep[0] = a0[...].astype(F32) + ra[0].astype(F32)
        to_b[...] = (a1[...].astype(F32) + ra[1].astype(F32)).astype(BF)
        keep[1] = b0[...].astype(F32) + rb[0].astype(F32)
        to_a[...] = (b1[...].astype(F32) + rb[1].astype(F32)).astype(BF)

    pair = pl.BlockSpec((2, rows, unit), lambda g, ids: (0, 0, g))
    flat = pl.BlockSpec((rows, unit), lambda g, ids: (0, g))
    return pl.pallas_call(
        kernel,
        grid_spec=pltpu.PrefetchScalarGridSpec(
            num_scalar_prefetch=1,
            grid=(n // unit,),
            in_specs=[spec(0), spec(1), spec(2), spec(3), pair, pair],
            out_specs=[flat, flat, pair],
        ),
        out_shape=[
            jax.ShapeDtypeStruct((rows, n), BF),
            jax.ShapeDtypeStruct((rows, n), BF),
            jax.ShapeDtypeStruct((2, rows, n), F32),
        ],
        compiler_params=params(),
        cost_estimate=cost(4 * rows * n, 28 * rows * n),
    )(block_ids, partial, partial, partial, partial, from_a, from_b)


def second_add(inner, keep, from_a, from_b, residual, start):
    _, rows, n = keep.shape
    unit = 128
    first = start // unit

    def kernel(ids, keep, ra, rb, res, out, send):
        extra = res[...].astype(F32)
        zero = jnp.zeros_like(extra)
        left = keep[0] + rb[...].astype(F32) + jnp.where(ids[0] == 0, extra, zero)
        right = keep[1] + ra[...].astype(F32) + jnp.where(ids[0] == 1, extra, zero)
        out[0] = left
        out[1] = right
        send[0] = left.astype(BF)
        send[1] = right.astype(BF)

    pair = pl.BlockSpec((2, rows, unit), lambda g, ids: (0, 0, g))
    flat = pl.BlockSpec((rows, unit), lambda g, ids: (0, g))
    return pl.pallas_call(
        kernel,
        grid_spec=pltpu.PrefetchScalarGridSpec(
            num_scalar_prefetch=1,
            grid=(n // unit,),
            in_specs=[
                pair,
                flat,
                flat,
                pl.BlockSpec((rows, unit), lambda g, ids: (0, first + g)),
            ],
            out_specs=[pair, pair],
        ),
        out_shape=[
            jax.ShapeDtypeStruct((2, rows, n), F32),
            jax.ShapeDtypeStruct((2, rows, n), BF),
        ],
        compiler_params=params(),
        cost_estimate=cost(4 * rows * n, 26 * rows * n),
    )(inner, keep, from_a, from_b, residual)


def update(inner, local, arrived, gain, start):
    _, rows, n = local.shape
    unit = 128
    first = start // unit

    def kernel(ids, local, arrived, gain, stream, scaled, squares):
        both = (local[...] + arrived[...].astype(F32)).astype(BF)
        values = both.astype(F32)
        stream[...] = jnp.where(ids[0] == 0, values[0], values[1]).astype(BF)
        scaled[...] = (values * gain[...]).astype(BF)
        part = values[0] * values[0] + values[1] * values[1]

        @pl.when(pl.program_id(0) == 0)
        def _():
            squares[...] = part

        @pl.when(pl.program_id(0) > 0)
        def _():
            squares[...] += part

    pair = pl.BlockSpec((2, rows, unit), lambda g, ids: (0, 0, g))
    flat = pl.BlockSpec((rows, unit), lambda g, ids: (0, g))
    return pl.pallas_call(
        kernel,
        grid_spec=pltpu.PrefetchScalarGridSpec(
            num_scalar_prefetch=1,
            grid=(n // unit,),
            in_specs=[
                pair,
                pair,
                pl.BlockSpec((2, 1, unit), lambda g, ids: (0, 0, first + g)),
            ],
            out_specs=[
                flat,
                pair,
                pl.BlockSpec((rows, unit), lambda g, ids: (0, 0)),
            ],
        ),
        out_shape=[
            jax.ShapeDtypeStruct((rows, n), BF),
            jax.ShapeDtypeStruct((2, rows, n), BF),
            jax.ShapeDtypeStruct((rows, unit), F32),
        ],
        compiler_params=params(),
        cost_estimate=cost(8 * rows * n, 20 * rows * n),
    )(inner, local, arrived, gain)


def pick_weights(weight, row_ids):
    pair = weight.shape[1]

    def spec(t):
        return pl.BlockSpec((UNIT, pair), lambda g, ids: (ids[t], 0))

    def kernel(ids, *refs):
        for j in range(3):
            refs[6 + j][0] = refs[2 * j][...]
            refs[6 + j][1] = refs[2 * j + 1][...]

    return pl.pallas_call(
        kernel,
        grid_spec=pltpu.PrefetchScalarGridSpec(
            num_scalar_prefetch=1,
            grid=(1,),
            in_specs=[spec(t) for t in range(6)],
            out_specs=[
                pl.BlockSpec((2, UNIT, pair), lambda g, ids: (0, 0, 0))
                for _ in range(3)
            ],
        ),
        out_shape=[jax.ShapeDtypeStruct((2, UNIT, pair), BF)] * 3,
        compiler_params=params(),
        cost_estimate=cost(0, 24 * UNIT * pair),
    )(row_ids, *([weight] * 6))


def project(own_rows, scaled, squares, gathered, weight):
    rows = scaled[0].shape[1]
    pair = weight.shape[1]
    units = gathered.shape[0]
    n_chunk = len(scaled)

    def kernel(ids, *refs):
        xs = refs[:n_chunk]
        sq = refs[n_chunk : 2 * n_chunk]
        far, near = refs[2 * n_chunk : 2 * n_chunk + 2]
        m1, m2, m3, own, total, far_buf, near_buf, far_sem, near_sem = refs[
            2 * n_chunk + 2 :
        ]
        copies = []
        for q in range(units):
            one = pltpu.make_async_copy(far.at[q], far_buf.at[q], far_sem.at[q])
            one.start()
            two = []
            for i in range(2):
                at = pl.multiple_of(ids[i] + q * UNIT, UNIT)
                c = pltpu.make_async_copy(
                    near.at[pl.ds(at, UNIT), :], near_buf.at[q, i], near_sem.at[q, i]
                )
                c.start()
                two.append(c)
            copies.append([one] + two)
        acc = [jnp.zeros((rows, pair), F32) for _ in range(4)]
        q = 0
        for x in xs:
            for u in range(x.shape[2] // 128):
                pass
        spans = []
        for x_id, x in enumerate(xs):
            at = 0
            while at < x.shape[2]:
                here = sum(xs[t].shape[2] for t in range(x_id)) + at
                room = UNIT - here % UNIT
                size = min(room, x.shape[2] - at)
                spans.append((x_id, at, here // UNIT, here % UNIT, size))
                at += size
        waited = set()
        for x_id, at, q, inside, size in spans:
            if q not in waited:
                for c in copies[q]:
                    c.wait()
                waited.add(q)
            for i in range(2):
                value = xs[x_id][i, :, at : at + size]
                acc[0] += jnp.dot(
                    value,
                    near_buf[q, i, inside : inside + size, :],
                    preferred_element_type=F32,
                )
                for k in range(3):
                    acc[k + 1] += jnp.dot(
                        value,
                        far_buf[q, k, i, inside : inside + size, :],
                        preferred_element_type=F32,
                    )
        lanes = sq[0][...]
        for other in sq[1:]:
            lanes = lanes + other[...]
        whole = jnp.sum(lanes, axis=1, keepdims=True)
        own[...] = acc[0]
        total[...] = jnp.broadcast_to(whole, total.shape)
        high = whole.astype(BF)
        low = (whole - high.astype(F32)).astype(BF)
        lane = lax.broadcasted_iota(jnp.int32, (rows, 128), 1)
        tail = jnp.where(lane < 64, high.astype(F32), low.astype(F32)).astype(BF)
        for k, m in enumerate((m1, m2, m3)):
            m[:, :pair] = acc[k + 1].astype(BF)
            m[:, pair:] = tail

    return pl.pallas_call(
        kernel,
        in_specs=[SMEM] + [VMEM] * (2 * n_chunk) + [ANY, ANY],
        out_specs=[VMEM] * 5,
        out_shape=[jax.ShapeDtypeStruct((rows, pair + 128), BF)] * 3
        + [
            jax.ShapeDtypeStruct((rows, pair), F32),
            jax.ShapeDtypeStruct((rows, 128), F32),
        ],
        scratch_shapes=[
            pltpu.VMEM((units, 3, 2, UNIT, pair), BF),
            pltpu.VMEM((units, 2, UNIT, pair), BF),
            pltpu.SemaphoreType.DMA((units,)),
            pltpu.SemaphoreType.DMA((units, 2)),
        ],
        compiler_params=params(),
        cost_estimate=cost(2 * rows * 4096 * 1024, 10 * 1024 * 1024),
    )(own_rows, *scaled, *squares, gathered, weight)


def finish(own, total, arrived, width):
    rows, pair = own.shape

    def kernel(own, total, a, b, c, out):
        value = own[...]
        squares = total[:, :1]
        for m in (a, b, c):
            value = value + m[:, :pair].astype(F32)
            tail = m[:, pair:].astype(F32)
            squares = squares + tail[:, :1] + tail[:, 64:65]
        factor = lax.rsqrt(squares * (1.0 / width) + 1e-05)
        out[...] = (value * factor).astype(BF)

    return pl.pallas_call(
        kernel,
        in_specs=[VMEM] * 5,
        out_specs=VMEM,
        out_shape=jax.ShapeDtypeStruct((rows, pair), BF),
        compiler_params=params(),
        cost_estimate=cost(8 * rows * pair, 12 * rows * pair),
    )(own, total, *arrived)


def body(partials, residual, norm_gain, kv_weight):
    partial = partials[0]
    rows, width = partial.shape
    pair = kv_weight.shape[2]
    weight = kv_weight.reshape(width, pair)
    o = lax.axis_index("outer").astype(jnp.int32)
    i = lax.axis_index("inner").astype(jnp.int32)
    q = (lax.axis_index("x") * 2 + lax.axis_index("core")).astype(jnp.int32)
    inner = i.reshape(1)
    block = width // 8
    per_block = block // UNIT

    ids = []
    for k in (1, 2, 3):
        there = (o + k) % OUTER
        ids += [there * per_block + q, (OUTER + there) * per_block + q]
    sent = pick_weights(weight, jnp.stack(ids))
    got = [lax.ppermute(s, "outer", shift(k)) for k, s in zip((1, 2, 3), sent)]
    gathered = lax.all_gather(jnp.stack(got), ("x", "core"), axis=0)

    send_ids = jnp.stack([o ^ 1, o ^ 2, OUTER + (o ^ 3), OUTER + (o ^ 2)])
    keep_ids = jnp.stack([o, o ^ 3, OUTER + o, OUTER + (o ^ 1)])
    gain = lax.dynamic_index_in_dim(
        norm_gain.reshape(2, OUTER, block), o, 1, keepdims=True
    )
    streams, scaled, squares = [], [], []
    start = 0
    for n in CHUNKS:
        to_a, to_b = pick_columns(partial, send_ids, n, start, 2)
        from_a = lax.ppermute(to_a, "outer", PAIR_A)
        from_b = lax.ppermute(to_b, "outer", PAIR_B)
        to_a, to_b, keep = first_add(partial, keep_ids, from_a, from_b, start)
        from_a = lax.ppermute(to_a, "outer", PAIR_A)
        from_b = lax.ppermute(to_b, "outer", PAIR_B)
        local, to_z = second_add(inner, keep, from_a, from_b, residual, start)
        from_z = lax.ppermute(to_z, "inner", SWAP)
        s, x, sq = update(inner, local, from_z, gain, start)
        streams.append(s)
        scaled.append(x)
        squares.append(sq)
        start += n

    own_rows = jnp.stack([o * block, (OUTER + o) * block])
    *messages, own, total = project(own_rows, scaled, squares, gathered, weight)
    arrived = [
        lax.ppermute(m, "outer", shift(-k)) for k, m in zip((1, 2, 3), messages)
    ]
    kv = finish(own, total, arrived, width)
    stream = jnp.concatenate(streams, axis=1)
    return stream, kv.reshape(rows, 1, pair)


def solution(mesh):
    fine = Mesh(
        mesh.devices.reshape(4, 4, 2, 2, 4), ("x", "z_lo", "core", "inner", "outer")
    )
    dp = ("x", "z_lo", "core")
    placed = (
        P((*dp, "inner", "outer"), None, None),
        P(dp, ("inner", "outer")),
        P(),
        P(None, ("inner", "outer"), None),
    )
    return jax.shard_map(
        body,
        mesh=fine,
        in_specs=placed,
        out_specs=(P(dp, ("inner", "outer")), P(dp, ("inner", "outer"), None)),
        check_vma=False,
    )
```

```python
import jax
import jax.numpy as jnp
from jax import lax
from jax.experimental import pallas as pl
from jax.experimental.pallas import tpu as pltpu
from jax.sharding import Mesh
from jax.sharding import PartitionSpec as P

BF = jnp.bfloat16
F32 = jnp.float32
OUTER = 4
UNIT = 256
CHUNKS = ((0, 512), (512, 896), (1408, 640))
ANY = pl.BlockSpec(memory_space=pl.ANY)
HBM = pl.BlockSpec(memory_space=pltpu.HBM)
VMEM = pl.BlockSpec(memory_space=pltpu.VMEM)
SMEM = pl.BlockSpec(memory_space=pltpu.SMEM)
PAIR_A = [(o, o ^ 1) for o in range(4)]
PAIR_B = [(o, o ^ 3) for o in range(4)]
SWAP = [(0, 1), (1, 0)]
MB = 1024 * 1024
COSTS = (12.0, 10.0, 10.0, 12.0)
COPY = pltpu.SemaphoreType.DMA


def shift(k):
    return [(o, (o + k) % 4) for o in range(4)]


def sds(*shape, dtype=BF):
    return pltpu.VMEM(shape, dtype)


def pin(*arrays):
    return [pltpu.with_memory_space_constraint(a, pltpu.HBM) for a in arrays]


def call(
    name, kernel, ids, args, in_specs, out_shape, scratch=(), after=(), mb=4, out_specs=None
):
    share = 0.0
    if after and isinstance(after[-1], float):
        *after, share = after
    in_specs = [SMEM, *in_specs] + [ANY] * len(after)
    args = [ids, *args, *after]
    inner = kernel
    spot = len(args) - len(after)

    def kernel(*refs):
        inner(*refs[:spot], *refs[len(args) :])

    return pl.pallas_call(
        kernel,
        in_specs=in_specs,
        out_specs=out_specs or [VMEM] * len(out_shape),
        out_shape=out_shape,
        scratch_shapes=list(scratch),
        compiler_params=pltpu.CompilerParams(vmem_limit_bytes=mb * MB),
        cost_estimate=pl.CostEstimate(
            flops=int(share * 1e9), bytes_accessed=int(share * MB), transcendentals=0
        ),
        name=name,
    )(*args)


def run(copies):
    for c in copies:
        c.start()
    for c in copies:
        c.wait()


def pick_columns(ids, partial, chunk, after=()):
    rows, width = partial.shape
    start, n = chunk
    block = width // 8

    def kernel(ids, src, to_a, to_b, own, sem):
        o = ids[1]
        run(
            [
                pltpu.make_async_copy(
                    src.at[
                        :, pl.ds(pl.multiple_of((half + there) * block + start, 128), n)
                    ],
                    out.at[slot],
                    sem.at[t],
                )
                for t, (out, slot, half, there) in enumerate(
                    (
                        (to_a, 0, 0, o ^ 1),
                        (to_a, 1, 0, o ^ 2),
                        (to_b, 0, OUTER, o ^ 3),
                        (to_b, 1, OUTER, o ^ 2),
                        (own, 0, 0, o),
                        (own, 1, 0, o ^ 3),
                        (own, 2, OUTER, o),
                        (own, 3, OUTER, o ^ 1),
                    )
                )
            ]
        )

    return call(
        "pick_columns",
        kernel,
        ids,
        (partial,),
        [HBM],
        [sds(2, rows, n), sds(2, rows, n), sds(4, rows, n)],
        [COPY((8,))],
        after,
    )


def first_add(ids, own, from_a, from_b, after=()):
    _, rows, n = own.shape

    def kernel(ids, own, ra, rb, to_a, to_b, keep):
        to_b[...] = (own[1].astype(F32) + ra[1].astype(F32)).astype(BF)
        to_a[...] = (own[3].astype(F32) + rb[1].astype(F32)).astype(BF)
        keep[0] = own[0].astype(F32) + ra[0].astype(F32)
        keep[1] = own[2].astype(F32) + rb[0].astype(F32)

    return call(
        "first_add",
        kernel,
        ids,
        (own, from_a, from_b),
        [VMEM] * 3,
        [sds(rows, n), sds(rows, n), sds(2, rows, n, dtype=F32)],
        after=after,
    )


def second_add(ids, keep, from_a, from_b, residual, chunk, after=()):
    _, rows, n = keep.shape
    start = chunk[0]

    def kernel(ids, keep, ra, rb, res, out, send):
        extra = res[:, start : start + n].astype(F32)
        zero = jnp.zeros_like(extra)
        left = keep[0] + rb[...].astype(F32) + jnp.where(ids[0] == 0, extra, zero)
        right = keep[1] + ra[...].astype(F32) + jnp.where(ids[0] == 1, extra, zero)
        out[0] = left
        out[1] = right
        send[0] = left.astype(BF)
        send[1] = right.astype(BF)

    return call(
        "second_add",
        kernel,
        ids,
        (keep, from_a, from_b, residual),
        [VMEM] * 4,
        [sds(2, rows, n, dtype=F32), sds(2, rows, n)],
        after=after,
    )


def update(ids, local, arrived, gain, chunk, after=()):
    _, rows, n = local.shape
    start = chunk[0]
    block = gain.shape[0] // 8

    def kernel(ids, local, arrived, gain, stream, scaled, squares):
        mine = ids[0] == 0
        part = jnp.zeros((rows, 128), F32)
        for u in range(n // 128):
            at = slice(u * 128, (u + 1) * 128)
            values = []
            for i in range(2):
                row = (i * OUTER + ids[1]) * block + start // 128 + u
                value = (local[i, :, at] + arrived[i, :, at].astype(F32)).astype(BF)
                wide = value.astype(F32)
                scaled[i, :, at] = (wide * gain[pl.ds(row, 1), :]).astype(BF)
                part = part + wide * wide
                values.append(wide)
            stream[:, at] = jnp.where(mine, values[0], values[1]).astype(BF)
        squares[...] = part

    return call(
        "update",
        kernel,
        ids,
        (local, arrived, gain),
        [VMEM] * 3,
        [sds(rows, n), sds(2, rows, n), sds(rows, 128, dtype=F32)],
        after=after,
    )


def pick_weights(ids, weight, after=()):
    width, pair = weight.shape
    block = width // 8

    def kernel(ids, src, *refs):
        outs, sem = refs[:3], refs[3]
        q = ids[2] * 2 + ids[3]
        copies = []
        for k in range(3):
            there = lax.rem(ids[1] + k + 1, OUTER)
            for i in range(2):
                at = pl.multiple_of((i * OUTER + there) * block + q * UNIT, UNIT)
                copies.append(
                    pltpu.make_async_copy(
                        src.at[pl.ds(at, UNIT), :], outs[k].at[i], sem.at[2 * k + i]
                    )
                )
        run(copies)

    return call(
        "pick_weights",
        kernel,
        ids,
        (weight,),
        [HBM],
        [sds(2, UNIT, pair)] * 3,
        [COPY((6,))],
        after,
    )


def stack(ids, pieces, after=()):
    shape = pieces[0].shape

    def kernel(ids, a, b, c, out, sem):
        run(
            [
                pltpu.make_async_copy(src, out.at[k], sem.at[k])
                for k, src in enumerate((a, b, c))
            ]
        )

    return call(
        "stack",
        kernel,
        ids,
        pieces,
        [VMEM] * 3,
        [sds(3, *shape)],
        [COPY((3,))],
        after,
    )[0]


def project(ids, streams, scaled, squares, pieces, weight):
    rows = scaled[0].shape[1]
    width, pair = weight.shape
    block = width // 8
    n_chunk = len(scaled)
    shifts = (0, 1, 2, 3, 0, 1, 3)

    def kernel(ids, *refs):
        refs = list(refs)

        def take(count):
            taken = refs[:count]
            del refs[:count]
            return taken

        ys, xs, sq = take(n_chunk), take(n_chunk), take(n_chunk)
        pieces = take(7)
        (mine,) = take(1)
        some, own, total, stream = take(4)
        x_buf, mine_buf, y_sem, x_sem, mine_sem = refs
        copies = [
            pltpu.make_async_copy(
                mine.at[
                    pl.ds(pl.multiple_of((i * OUTER + ids[1]) * block, block), block), :
                ],
                mine_buf.at[i],
                mine_sem.at[i],
            )
            for i in range(2)
        ]
        moves = [
            pltpu.make_async_copy(x, x_buf.at[:, :, pl.ds(start, n)], x_sem.at[t])
            for t, (x, (start, n)) in enumerate(zip(xs, CHUNKS))
        ]
        leave = [
            pltpu.make_async_copy(y, stream.at[:, pl.ds(start, n)], y_sem.at[t])
            for t, (y, (start, n)) in enumerate(zip(ys, CHUNKS))
        ]
        for c in moves + copies + leave:
            c.start()
        lanes = sq[0][...]
        for more in sq[1:]:
            lanes = lanes + more[...]
        whole_sum = jnp.sum(lanes, axis=1, keepdims=True)
        total[...] = jnp.broadcast_to(whole_sum, total.shape)
        for c in moves:
            c.wait()
        acc = [jnp.zeros((rows, pair), F32) for _ in range(3)]
        for t, piece in enumerate(pieces):
            core = ids[3] if t < 4 else 1 - ids[3]
            source = lax.rem(ids[2] + 4 - shifts[t], 4)
            at = pl.multiple_of((2 * source + core) * UNIT, UNIT)
            for i in range(2):
                value = x_buf[i, :, pl.ds(at, UNIT)]
                for k in range(3):
                    acc[k] += jnp.dot(value, piece[k, i], preferred_element_type=F32)
        for k in range(3):
            some[k] = acc[k]
        for c in copies:
            c.wait()
        own[...] = jnp.dot(
            x_buf[0], mine_buf[0], preferred_element_type=F32
        ) + jnp.dot(x_buf[1], mine_buf[1], preferred_element_type=F32)
        for c in leave:
            c.wait()

    return call(
        "project",
        kernel,
        ids,
        (*streams, *scaled, *squares, *pieces, weight),
        [VMEM] * (3 * n_chunk + 7) + [HBM],
        [
            sds(3, rows, pair, dtype=F32),
            sds(rows, pair, dtype=F32),
            sds(rows, 128, dtype=F32),
            jax.ShapeDtypeStruct((rows, block), BF),
        ],
        [
            pltpu.VMEM((2, rows, block), BF),
            pltpu.VMEM((2, block, pair), BF),
            COPY((n_chunk,)),
            COPY((n_chunk,)),
            COPY((2,)),
        ],
        mb=8,
        out_specs=[VMEM] * 3 + [ANY],
    )


def complete(ids, some, total, scaled, piece):
    _, rows, pair = some.shape
    n_chunk = len(scaled)
    block = sum(n for _, n in CHUNKS)

    def kernel(ids, some, total, *refs):
        xs = refs[:n_chunk]
        piece, *messages, x_buf, x_sem = refs[n_chunk:]
        moves = [
            pltpu.make_async_copy(x, x_buf.at[:, :, pl.ds(start, n)], x_sem.at[t])
            for t, (x, (start, n)) in enumerate(zip(xs, CHUNKS))
        ]
        for c in moves:
            c.start()
        whole_sum = total[:, :1]
        high = whole_sum.astype(BF)
        low = (whole_sum - high.astype(F32)).astype(BF)
        lane = lax.broadcasted_iota(jnp.int32, (rows, 128), 1)
        tail = jnp.where(lane < 64, high.astype(F32), low.astype(F32)).astype(BF)
        for m in messages:
            m[:, pair:] = tail
        for c in moves:
            c.wait()
        source = lax.rem(ids[2] + 2, 4)
        at = pl.multiple_of((2 * source + 1 - ids[3]) * UNIT, UNIT)
        left, right = x_buf[0, :, pl.ds(at, UNIT)], x_buf[1, :, pl.ds(at, UNIT)]
        for k, m in enumerate(messages):
            value = (
                some[k]
                + jnp.dot(left, piece[k, 0], preferred_element_type=F32)
                + jnp.dot(right, piece[k, 1], preferred_element_type=F32)
            )
            m[:, :pair] = value.astype(BF)

    return call(
        "complete",
        kernel,
        ids,
        (some, total, *scaled, piece),
        [VMEM] * (3 + n_chunk),
        [sds(rows, pair + 128)] * 3,
        [pltpu.VMEM((2, rows, block), BF), COPY((n_chunk,))],
    )


def finish(ids, own, total, arrived, width):
    rows, pair = own.shape

    def kernel(ids, own, total, a, b, c, out):
        value = own[...]
        squares = total[:, :1]
        for m in (a, b, c):
            value = value + m[:, :pair].astype(F32)
            tail = m[:, pair:].astype(F32)
            squares = squares + tail[:, :1] + tail[:, 64:65]
        factor = lax.rsqrt(squares * (1.0 / width) + 1e-05)
        out[...] = (value * factor).astype(BF)

    return call(
        "finish",
        kernel,
        ids,
        (own, total, *arrived),
        [VMEM] * 5,
        [jax.ShapeDtypeStruct((rows, pair), BF)],
    )[0]


def gate(ids, value, *after):
    def kernel(*refs):
        pass

    return pl.pallas_call(
        kernel,
        in_specs=[SMEM, ANY] + [ANY] * len(after),
        out_specs=ANY,
        out_shape=jax.ShapeDtypeStruct(value.shape, value.dtype),
        input_output_aliases={1: 0},
        compiler_params=pltpu.CompilerParams(vmem_limit_bytes=4 * MB),
        cost_estimate=pl.CostEstimate(flops=0, bytes_accessed=0, transcendentals=0),
    )(ids, value, *after)


def body(partials, residual, norm_gain, kv_weight):
    partial = partials[0]
    rows, width = partial.shape
    pair = kv_weight.shape[2]
    weight = kv_weight.reshape(width, pair)
    partial, weight = pin(partial, weight)
    ids = jnp.stack(
        [lax.axis_index(a).astype(jnp.int32) for a in ("inner", "outer", "x", "core")]
    )
    gain = norm_gain.reshape(width // 128, 128)

    def send(label, value, axis, pairs):
        with jax.named_scope(label):
            return lax.ppermute(value, axis, pairs)

    def cross(label, pair):
        return (
            send(label + "_a", pair[0], "outer", PAIR_A),
            send(label + "_b", pair[1], "outer", PAIR_B),
        )

    c0, c1, c2 = CHUNKS
    *p0, own0 = pick_columns(ids, partial, c0)
    r0 = cross("first0", p0)
    sent = pick_weights(ids, weight, [own0])
    got = [send(f"weights{k}", s, "outer", shift(k)) for k, s in zip((1, 2, 3), sent)]
    *f0, keep0 = first_add(ids, own0, *r0, [sent[0]])
    r0 = cross("second0", f0)
    local0, z0 = second_add(ids, keep0, *r0, residual, c0)
    z0 = send("inner0", z0, "inner", SWAP)
    *p1, own1 = pick_columns(ids, partial, c1, [local0])
    r1 = cross("first1", p1)
    near0 = stack(ids, got, [own1, COSTS[3]])
    near1 = send("along_x1", near0, "x", shift(1))
    near3 = send("along_x3", near0, "x", shift(3))
    *f1, keep1 = first_add(ids, own1, *r1, [near0])
    r1 = cross("second1", f1)
    stream0, scaled0, squares0 = update(ids, local0, z0, gain, c0, [keep1, COSTS[0]])
    local1, z1 = second_add(ids, keep1, *r1, residual, c1, [stream0])
    z1 = send("inner1", z1, "inner", SWAP)
    *p2, own2 = pick_columns(ids, partial, c2, [local1])
    r2 = cross("first2", p2)
    near0 = gate(ids, near0, near1, near3)
    near2 = send("along_x2", near0, "x", shift(2))
    *f2, keep2 = first_add(ids, own2, *r2, [own2])
    r2 = cross("second2", f2)
    local2, z2 = second_add(ids, keep2, *r2, residual, c2)
    z2 = send("inner2", z2, "inner", SWAP)
    far0 = send("core0", near0, "core", SWAP)
    far1 = send("core1", near1, "core", SWAP)
    far3 = send("core3", near3, "core", SWAP)
    stream1, scaled1, squares1 = update(ids, local1, z1, gain, c1, [local2, COSTS[1]])
    stream2, scaled2, squares2 = update(ids, local2, z2, gain, c2, [stream1, COSTS[2]])
    far2 = send("core2", near2, "core", SWAP)
    some, own, total, stream = project(
        ids,
        [stream0, stream1, stream2],
        [scaled0, scaled1, scaled2],
        [squares0, squares1, squares2],
        [near0, near1, near2, near3, far0, far1, far3],
        weight,
    )
    messages = complete(ids, some, total, [scaled0, scaled1, scaled2], far2)
    arrived = [
        send(f"products{k}", m, "outer", shift(-k)) for k, m in zip((1, 2, 3), messages)
    ]
    kv = finish(ids, own, total, arrived, width)
    return stream, kv.reshape(rows, 1, pair)


def solution(mesh):
    fine = Mesh(
        mesh.devices.reshape(4, 4, 2, 2, 4), ("x", "z_lo", "core", "inner", "outer")
    )
    dp = ("x", "z_lo", "core")
    placed = (
        P((*dp, "inner", "outer"), None, None),
        P(dp, ("inner", "outer")),
        P(),
        P(None, ("inner", "outer"), None),
    )
    return jax.shard_map(
        body,
        mesh=fine,
        in_specs=placed,
        out_specs=(P(dp, ("inner", "outer")), P(dp, ("inner", "outer"), None)),
        check_vma=False,
    )
```

```python
import jax
import jax.numpy as jnp
from jax import lax
from jax.experimental import pallas as pl
from jax.experimental.pallas import tpu as pltpu
from jax.sharding import Mesh
from jax.sharding import PartitionSpec as P

BF = jnp.bfloat16
F32 = jnp.float32
OUTER = 4
UNIT = 256
CHUNKS = ((0, 640), (640, 896), (1536, 512))
ANY = pl.BlockSpec(memory_space=pl.ANY)
HBM = pl.BlockSpec(memory_space=pltpu.HBM)
VMEM = pl.BlockSpec(memory_space=pltpu.VMEM)
SMEM = pl.BlockSpec(memory_space=pltpu.SMEM)
PAIR_A = [(o, o ^ 1) for o in range(4)]
PAIR_B = [(o, o ^ 3) for o in range(4)]
SWAP = [(0, 1), (1, 0)]
MB = 1024 * 1024
COSTS = (0.0, 8.0, 0.0, 0.0, 0.0, 0.0, 0.0, 10.0, 0.0, 5.0, 5.0)
COPY = pltpu.SemaphoreType.DMA


def shift(k):
    return [(o, (o + k) % 4) for o in range(4)]


def sds(*shape, dtype=BF):
    return pltpu.VMEM(shape, dtype)


def pin(*arrays):
    return [pltpu.with_memory_space_constraint(a, pltpu.HBM) for a in arrays]


def call(
    name, kernel, ids, args, in_specs, out_shape, scratch=(), after=(), mb=4, out_specs=None
):
    share = 0.0
    if after and isinstance(after[-1], float):
        *after, share = after
    in_specs = [SMEM, *in_specs] + [ANY] * len(after)
    args = [ids, *args, *after]
    inner = kernel
    spot = len(args) - len(after)

    def kernel(*refs):
        inner(*refs[:spot], *refs[len(args) :])

    return pl.pallas_call(
        kernel,
        in_specs=in_specs,
        out_specs=out_specs or [VMEM] * len(out_shape),
        out_shape=out_shape,
        scratch_shapes=list(scratch),
        compiler_params=pltpu.CompilerParams(vmem_limit_bytes=mb * MB),
        cost_estimate=pl.CostEstimate(
            flops=int(share * 1e9), bytes_accessed=int(share * MB), transcendentals=0
        ),
        name=name,
    )(*args)


def run(copies):
    for c in copies:
        c.start()
    for c in copies:
        c.wait()


def pick_columns(ids, partial, chunk, after=()):
    rows, width = partial.shape
    start, n = chunk
    block = width // 8

    def kernel(ids, src, to_a, to_b, own, sem):
        o = ids[1]
        run(
            [
                pltpu.make_async_copy(
                    src.at[
                        :, pl.ds(pl.multiple_of((half + there) * block + start, 128), n)
                    ],
                    out.at[slot],
                    sem.at[t],
                )
                for t, (out, slot, half, there) in enumerate(
                    (
                        (to_a, 0, 0, o ^ 1),
                        (to_a, 1, 0, o ^ 2),
                        (to_b, 0, OUTER, o ^ 3),
                        (to_b, 1, OUTER, o ^ 2),
                        (own, 0, 0, o),
                        (own, 1, 0, o ^ 3),
                        (own, 2, OUTER, o),
                        (own, 3, OUTER, o ^ 1),
                    )
                )
            ]
        )

    return call(
        "pick_columns",
        kernel,
        ids,
        (partial,),
        [HBM],
        [sds(2, rows, n), sds(2, rows, n), sds(4, rows, n)],
        [COPY((8,))],
        after,
    )


def first_add(ids, own, from_a, from_b, after=()):
    _, rows, n = own.shape

    def kernel(ids, own, ra, rb, to_a, to_b, keep):
        to_b[...] = (own[1].astype(F32) + ra[1].astype(F32)).astype(BF)
        to_a[...] = (own[3].astype(F32) + rb[1].astype(F32)).astype(BF)
        keep[0] = own[0].astype(F32) + ra[0].astype(F32)
        keep[1] = own[2].astype(F32) + rb[0].astype(F32)

    return call(
        "first_add",
        kernel,
        ids,
        (own, from_a, from_b),
        [VMEM] * 3,
        [sds(rows, n), sds(rows, n), sds(2, rows, n, dtype=F32)],
        after=after,
    )


def second_add(ids, keep, from_a, from_b, residual, chunk, after=()):
    _, rows, n = keep.shape
    start = chunk[0]

    def kernel(ids, keep, ra, rb, res, out, send):
        extra = res[:, start : start + n].astype(F32)
        zero = jnp.zeros_like(extra)
        left = keep[0] + rb[...].astype(F32) + jnp.where(ids[0] == 0, extra, zero)
        right = keep[1] + ra[...].astype(F32) + jnp.where(ids[0] == 1, extra, zero)
        out[0] = left
        out[1] = right
        send[0] = left.astype(BF)
        send[1] = right.astype(BF)

    return call(
        "second_add",
        kernel,
        ids,
        (keep, from_a, from_b, residual),
        [VMEM] * 4,
        [sds(2, rows, n, dtype=F32), sds(2, rows, n)],
        after=after,
    )


def update(ids, local, arrived, gain, chunk, after=()):
    _, rows, n = local.shape
    start = chunk[0]
    block = gain.shape[0] // 8

    def kernel(ids, local, arrived, gain, stream, scaled, squares):
        mine = ids[0] == 0
        part = jnp.zeros((rows, 128), F32)
        for u in range(n // 128):
            at = slice(u * 128, (u + 1) * 128)
            values = []
            for i in range(2):
                row = (i * OUTER + ids[1]) * block + start // 128 + u
                value = (local[i, :, at] + arrived[i, :, at].astype(F32)).astype(BF)
                wide = value.astype(F32)
                scaled[i, :, at] = (wide * gain[pl.ds(row, 1), :]).astype(BF)
                part = part + wide * wide
                values.append(wide)
            stream[:, at] = jnp.where(mine, values[0], values[1]).astype(BF)
        squares[...] = part

    return call(
        "update",
        kernel,
        ids,
        (local, arrived, gain),
        [VMEM] * 3,
        [sds(rows, n), sds(2, rows, n), sds(rows, 128, dtype=F32)],
        after=after,
    )


def pick_weights(ids, weight, after=()):
    width, pair = weight.shape
    block = width // 8

    def kernel(ids, src, *refs):
        outs, sem = refs[:3], refs[3]
        q = ids[2] * 2 + ids[3]
        copies = []
        for k in range(3):
            there = lax.rem(ids[1] + k + 1, OUTER)
            for i in range(2):
                at = pl.multiple_of((i * OUTER + there) * block + q * UNIT, UNIT)
                copies.append(
                    pltpu.make_async_copy(
                        src.at[pl.ds(at, UNIT), :], outs[k].at[i], sem.at[2 * k + i]
                    )
                )
        run(copies)

    return call(
        "pick_weights",
        kernel,
        ids,
        (weight,),
        [HBM],
        [sds(2, UNIT, pair)] * 3,
        [COPY((6,))],
        after,
    )


def stack(ids, pieces, after=()):
    shape = pieces[0].shape

    def kernel(ids, a, b, c, out):
        for k, src in enumerate((a, b, c)):
            for i in range(2):
                out[i, k] = src[i]

    return call(
        "stack",
        kernel,
        ids,
        pieces,
        [VMEM] * 3,
        [sds(2, 3, *shape[1:])],
        after=after,
    )[0]


def halves(ids, from_left, from_right, after=()):
    shape = from_left.shape[1:]

    def kernel(ids, a, b, left, right):
        left[...] = a[0]
        right[...] = b[1]

    return call(
        "halves",
        kernel,
        ids,
        (from_left, from_right),
        [VMEM] * 2,
        [sds(*shape), sds(*shape)],
        after=after,
    )


def project(ids, streams, scaled, squares, pieces, weight):
    rows = scaled[0].shape[1]
    width, pair = weight.shape
    block = width // 8
    n_chunk = len(scaled)
    plan = [p[1:] for p in pieces]
    pieces = [p[0] for p in pieces]

    def kernel(ids, *refs):
        refs = list(refs)

        def take(count):
            taken = refs[:count]
            del refs[:count]
            return taken

        ys, xs, sq = take(n_chunk), take(n_chunk), take(n_chunk)
        pieces = take(len(plan))
        (mine,) = take(1)
        some, own, total, stream = take(4)
        x_buf, mine_buf, y_sem, x_sem, mine_sem = refs
        copies = [
            pltpu.make_async_copy(
                mine.at[
                    pl.ds(pl.multiple_of((i * OUTER + ids[1]) * block, block), block), :
                ],
                mine_buf.at[i],
                mine_sem.at[i],
            )
            for i in range(2)
        ]
        moves = [
            pltpu.make_async_copy(x, x_buf.at[:, :, pl.ds(start, n)], x_sem.at[t])
            for t, (x, (start, n)) in enumerate(zip(xs, CHUNKS))
        ]
        leave = [
            pltpu.make_async_copy(y, stream.at[:, pl.ds(start, n)], y_sem.at[t])
            for t, (y, (start, n)) in enumerate(zip(ys, CHUNKS))
        ]
        for c in moves + copies + leave:
            c.start()
        lanes = sq[0][...]
        for more in sq[1:]:
            lanes = lanes + more[...]
        whole_sum = jnp.sum(lanes, axis=1, keepdims=True)
        total[...] = jnp.broadcast_to(whole_sum, total.shape)
        for c in moves:
            c.wait()
        acc = [jnp.zeros((rows, pair), F32) for _ in range(3)]
        for piece, (first, count, step, crossed) in zip(pieces, plan):
            for i in range(first, first + count):
                value = x_buf[i, :, columns_of(ids, step, crossed)]
                for k in range(3):
                    there = piece[k] if count == 1 else piece[i, k]
                    acc[k] += jnp.dot(value, there, preferred_element_type=F32)
        for k in range(3):
            some[k] = acc[k]
        for c in copies:
            c.wait()
        own[...] = jnp.dot(
            x_buf[0], mine_buf[0], preferred_element_type=F32
        ) + jnp.dot(x_buf[1], mine_buf[1], preferred_element_type=F32)
        for c in leave:
            c.wait()

    return call(
        "project",
        kernel,
        ids,
        (*streams, *scaled, *squares, *pieces, weight),
        [VMEM] * (3 * n_chunk + len(plan)) + [HBM],
        [
            sds(3, rows, pair, dtype=F32),
            sds(rows, pair, dtype=F32),
            sds(rows, 128, dtype=F32),
            jax.ShapeDtypeStruct((rows, block), BF),
        ],
        [
            pltpu.VMEM((2, rows, block), BF),
            pltpu.VMEM((2, block, pair), BF),
            COPY((n_chunk,)),
            COPY((n_chunk,)),
            COPY((2,)),
        ],
        mb=8,
        out_specs=[VMEM] * 3 + [ANY],
    )


def columns_of(ids, step, crossed):
    source = lax.rem(ids[2] + 4 - step, 4)
    core = 1 - ids[3] if crossed else ids[3]
    return pl.ds(pl.multiple_of((2 * source + core) * UNIT, UNIT), UNIT)


def complete(ids, some, total, scaled, pieces):
    _, rows, pair = some.shape
    n_chunk = len(scaled)
    block = sum(n for _, n in CHUNKS)

    def kernel(ids, some, total, *refs):
        xs = refs[:n_chunk]
        a, b, *messages, x_buf = refs[n_chunk:]
        for x, (start, n) in zip(xs, CHUNKS):
            x_buf[:, :, start : start + n] = x[...]
        whole_sum = total[:, :1]
        high = whole_sum.astype(BF)
        low = (whole_sum - high.astype(F32)).astype(BF)
        lane = lax.broadcasted_iota(jnp.int32, (rows, 128), 1)
        tail = jnp.where(lane < 64, high.astype(F32), low.astype(F32)).astype(BF)
        for m in messages:
            m[:, pair:] = tail
        left = x_buf[0, :, columns_of(ids, 2, True)]
        right = x_buf[1, :, columns_of(ids, 2, True)]
        for k, m in enumerate(messages):
            value = (
                some[k]
                + jnp.dot(left, a[k], preferred_element_type=F32)
                + jnp.dot(right, b[k], preferred_element_type=F32)
            )
            m[:, :pair] = value.astype(BF)

    return call(
        "complete",
        kernel,
        ids,
        (some, total, *scaled, *pieces),
        [VMEM] * (4 + n_chunk),
        [sds(rows, pair + 128)] * 3,
        [pltpu.VMEM((2, rows, block), BF)],
    )


def finish(ids, own, total, arrived, width):
    rows, pair = own.shape

    def kernel(ids, own, total, a, b, c, out):
        value = own[...]
        squares = total[:, :1]
        for m in (a, b, c):
            value = value + m[:, :pair].astype(F32)
            tail = m[:, pair:].astype(F32)
            squares = squares + tail[:, :1] + tail[:, 64:65]
        factor = lax.rsqrt(squares * (1.0 / width) + 1e-05)
        out[...] = (value * factor).astype(BF)

    return call(
        "finish",
        kernel,
        ids,
        (own, total, *arrived),
        [VMEM] * 5,
        [jax.ShapeDtypeStruct((rows, pair), BF)],
    )[0]


def body(partials, residual, norm_gain, kv_weight):
    partial = partials[0]
    rows, width = partial.shape
    pair = kv_weight.shape[2]
    weight = kv_weight.reshape(width, pair)
    partial, weight = pin(partial, weight)
    ids = jnp.stack(
        [lax.axis_index(a).astype(jnp.int32) for a in ("inner", "outer", "x", "core")]
    )
    gain = norm_gain.reshape(width // 128, 128)

    def send(label, value, axis, pairs):
        with jax.named_scope(label):
            return lax.ppermute(value, axis, pairs)

    def cross(label, pair):
        return (
            send(label + "_a", pair[0], "outer", PAIR_A),
            send(label + "_b", pair[1], "outer", PAIR_B),
        )

    c0, c1, c2 = CHUNKS
    *p0, own0 = pick_columns(ids, partial, c0)
    r0 = cross("first0", p0)
    *p1, own1 = pick_columns(ids, partial, c1, [own0, COSTS[0]])
    r1 = cross("first1", p1)
    *f0, keep0 = first_add(ids, own0, *r0, [own1, COSTS[1]])
    r0 = cross("second0", f0)
    local0, z0 = second_add(ids, keep0, *r0, residual, c0, [keep0, COSTS[2]])
    z0 = send("inner0", z0, "inner", SWAP)
    *f1, keep1 = first_add(ids, own1, *r1, [local0, COSTS[3]])
    r1 = cross("second1", f1)
    sent = pick_weights(ids, weight, [keep1])
    got = [send(f"weights{k}", s, "outer", shift(k)) for k, s in zip((1, 2, 3), sent)]
    local1, z1 = second_add(ids, keep1, *r1, residual, c1, [sent[0], COSTS[4]])
    z1 = send("inner1", z1, "inner", SWAP)
    *p2, own2 = pick_columns(ids, partial, c2, [local1])
    r2 = cross("first2", p2)
    stream0, scaled0, squares0 = update(ids, local0, z0, gain, c0, [own2, COSTS[5]])
    near0 = stack(ids, got, [stream0, COSTS[6]])
    near1 = send("along_x1", near0, "x", shift(1))
    near3 = send("along_x3", near0, "x", shift(3))
    *f2, keep2 = first_add(ids, own2, *r2, [near0, COSTS[7]])
    r2 = cross("second2", f2)
    local2, z2 = second_add(ids, keep2, *r2, residual, c2, [keep2, COSTS[8]])
    z2 = send("inner2", z2, "inner", SWAP)
    left, right = halves(ids, near1, near3)
    near2a = send("along_x2a", left, "x", shift(1))
    near2b = send("along_x2b", right, "x", shift(3))
    stream1, scaled1, squares1 = update(ids, local1, z1, gain, c1, [local2, COSTS[9]])
    stream2, scaled2, squares2 = update(ids, local2, z2, gain, c2, [stream1, COSTS[10]])
    far0, far1, far2a, far2b, far3 = [
        send(f"core{k}", w, "core", SWAP)
        for k, w in (("0", near0), ("1", near1), ("2a", near2a), ("2b", near2b), ("3", near3))
    ]
    some, own, total, stream = project(
        ids,
        [stream0, stream1, stream2],
        [scaled0, scaled1, scaled2],
        [squares0, squares1, squares2],
        [
            (near0, 0, 2, 0, False),
            (near1, 0, 2, 1, False),
            (near3, 0, 2, 3, False),
            (near2a, 0, 1, 2, False),
            (near2b, 1, 1, 2, False),
            (far0, 0, 2, 0, True),
            (far1, 0, 2, 1, True),
            (far3, 0, 2, 3, True),
        ],
        weight,
    )
    messages = complete(ids, some, total, [scaled0, scaled1, scaled2], [far2a, far2b])
    arrived = [
        send(f"products{k}", m, "outer", shift(-k)) for k, m in zip((1, 2, 3), messages)
    ]
    kv = finish(ids, own, total, arrived, width)
    return stream, kv.reshape(rows, 1, pair)


def solution(mesh):
    fine = Mesh(
        mesh.devices.reshape(4, 4, 2, 2, 4), ("x", "z_lo", "core", "inner", "outer")
    )
    dp = ("x", "z_lo", "core")
    placed = (
        P((*dp, "inner", "outer"), None, None),
        P(dp, ("inner", "outer")),
        P(),
        P(None, ("inner", "outer"), None),
    )
    return jax.shard_map(
        body,
        mesh=fine,
        in_specs=placed,
        out_specs=(P(dp, ("inner", "outer")), P(dp, ("inner", "outer"), None)),
        check_vma=False,
    )
```

```python
import jax
import jax.numpy as jnp
from jax import lax
from jax.experimental import pallas as pl
from jax.experimental.pallas import tpu as pltpu
from jax.sharding import Mesh
from jax.sharding import PartitionSpec as P

BF = jnp.bfloat16
F32 = jnp.float32
OUTER = 4
UNIT = 256
CHUNKS = ((0, 1152), (1152, 896))
ANY = pl.BlockSpec(memory_space=pl.ANY)
HBM = pl.BlockSpec(memory_space=pltpu.HBM)
VMEM = pl.BlockSpec(memory_space=pltpu.VMEM)
SMEM = pl.BlockSpec(memory_space=pltpu.SMEM)
PAIR_A = [(o, o ^ 1) for o in range(4)]
PAIR_B = [(o, o ^ 3) for o in range(4)]
SWAP = [(0, 1), (1, 0)]
MB = 1024 * 1024
COSTS = (0.0, 2.0, 0.0, 12.0, 0.0, 0.0, 0.0, 4.0, 10.0)
COPY = pltpu.SemaphoreType.DMA


def shift(k):
    return [(o, (o + k) % 4) for o in range(4)]


def sds(*shape, dtype=BF):
    return pltpu.VMEM(shape, dtype)


def pin(*arrays):
    return [pltpu.with_memory_space_constraint(a, pltpu.HBM) for a in arrays]


def call(
    name, kernel, ids, args, in_specs, out_shape, scratch=(), after=(), mb=4, out_specs=None
):
    share = 0.0
    if after and isinstance(after[-1], float):
        *after, share = after
    in_specs = [SMEM, *in_specs] + [ANY] * len(after)
    args = [ids, *args, *after]
    inner = kernel
    spot = len(args) - len(after)

    def kernel(*refs):
        inner(*refs[:spot], *refs[len(args) :])

    return pl.pallas_call(
        kernel,
        in_specs=in_specs,
        out_specs=out_specs or [VMEM] * len(out_shape),
        out_shape=out_shape,
        scratch_shapes=list(scratch),
        compiler_params=pltpu.CompilerParams(vmem_limit_bytes=mb * MB),
        cost_estimate=pl.CostEstimate(
            flops=int(share * 1e9), bytes_accessed=int(share * MB), transcendentals=0
        ),
        name=name,
    )(*args)


def run(copies):
    for c in copies:
        c.start()
    for c in copies:
        c.wait()


def pick_columns(ids, partial, chunk, after=()):
    rows, width = partial.shape
    start, n = chunk
    block = width // 8

    def kernel(ids, src, to_a, to_b, own, sem):
        o = ids[1]
        run(
            [
                pltpu.make_async_copy(
                    src.at[
                        :, pl.ds(pl.multiple_of((half + there) * block + start, 128), n)
                    ],
                    out.at[slot],
                    sem.at[t],
                )
                for t, (out, slot, half, there) in enumerate(
                    (
                        (to_a, 0, 0, o ^ 1),
                        (to_a, 1, 0, o ^ 2),
                        (to_b, 0, OUTER, o ^ 3),
                        (to_b, 1, OUTER, o ^ 2),
                        (own, 0, 0, o),
                        (own, 1, 0, o ^ 3),
                        (own, 2, OUTER, o),
                        (own, 3, OUTER, o ^ 1),
                    )
                )
            ]
        )

    return call(
        "pick_columns",
        kernel,
        ids,
        (partial,),
        [HBM],
        [sds(2, rows, n), sds(2, rows, n), sds(4, rows, n)],
        [COPY((8,))],
        after,
    )


def first_add(ids, own, from_a, from_b, after=()):
    _, rows, n = own.shape

    def kernel(ids, own, ra, rb, to_a, to_b, keep):
        to_b[...] = (own[1].astype(F32) + ra[1].astype(F32)).astype(BF)
        to_a[...] = (own[3].astype(F32) + rb[1].astype(F32)).astype(BF)
        keep[0] = own[0].astype(F32) + ra[0].astype(F32)
        keep[1] = own[2].astype(F32) + rb[0].astype(F32)

    return call(
        "first_add",
        kernel,
        ids,
        (own, from_a, from_b),
        [VMEM] * 3,
        [sds(rows, n), sds(rows, n), sds(2, rows, n, dtype=F32)],
        after=after,
    )


def second_add(ids, keep, from_a, from_b, residual, chunk, after=()):
    _, rows, n = keep.shape
    start = chunk[0]

    def kernel(ids, keep, ra, rb, res, out, send):
        extra = res[:, start : start + n].astype(F32)
        zero = jnp.zeros_like(extra)
        left = keep[0] + rb[...].astype(F32) + jnp.where(ids[0] == 0, extra, zero)
        right = keep[1] + ra[...].astype(F32) + jnp.where(ids[0] == 1, extra, zero)
        out[0] = left
        out[1] = right
        send[0] = left.astype(BF)
        send[1] = right.astype(BF)

    return call(
        "second_add",
        kernel,
        ids,
        (keep, from_a, from_b, residual),
        [VMEM] * 4,
        [sds(2, rows, n, dtype=F32), sds(2, rows, n)],
        after=after,
    )


def update(ids, local, arrived, gain, chunk, after=()):
    _, rows, n = local.shape
    start = chunk[0]
    block = gain.shape[0] // 8

    def kernel(ids, local, arrived, gain, stream, scaled, squares):
        mine = ids[0] == 0
        part = jnp.zeros((rows, 128), F32)
        for u in range(n // 128):
            at = slice(u * 128, (u + 1) * 128)
            values = []
            for i in range(2):
                row = (i * OUTER + ids[1]) * block + start // 128 + u
                value = (local[i, :, at] + arrived[i, :, at].astype(F32)).astype(BF)
                wide = value.astype(F32)
                scaled[i, :, at] = (wide * gain[pl.ds(row, 1), :]).astype(BF)
                part = part + wide * wide
                values.append(wide)
            stream[:, at] = jnp.where(mine, values[0], values[1]).astype(BF)
        squares[...] = part

    return call(
        "update",
        kernel,
        ids,
        (local, arrived, gain),
        [VMEM] * 3,
        [sds(rows, n), sds(2, rows, n), sds(rows, 128, dtype=F32)],
        after=after,
    )


def pick_weights(ids, weight, after=()):
    width, pair = weight.shape
    block = width // 8

    def kernel(ids, src, *refs):
        outs, sem = refs[:3], refs[3]
        q = ids[2] * 2 + ids[3]
        copies = []
        for k in range(3):
            there = lax.rem(ids[1] + k + 1, OUTER)
            for i in range(2):
                at = pl.multiple_of((i * OUTER + there) * block + q * UNIT, UNIT)
                copies.append(
                    pltpu.make_async_copy(
                        src.at[pl.ds(at, UNIT), :], outs[k].at[i], sem.at[2 * k + i]
                    )
                )
        run(copies)

    return call(
        "pick_weights",
        kernel,
        ids,
        (weight,),
        [HBM],
        [sds(2, UNIT, pair)] * 3,
        [COPY((6,))],
        after,
    )


def stack(ids, pieces, after=()):
    shape = pieces[0].shape

    def kernel(ids, a, b, c, out):
        for k, src in enumerate((a, b, c)):
            for i in range(2):
                out[i, k] = src[i]

    return call(
        "stack",
        kernel,
        ids,
        pieces,
        [VMEM] * 3,
        [sds(2, 3, *shape[1:])],
        after=after,
    )[0]


def halves(ids, own, from_left, from_right, after=()):
    shape = from_left.shape[1:]

    def kernel(ids, own, a, b, left, right, across):
        left[...] = a[0]
        right[...] = b[1]
        across[...] = own[...]

    return call(
        "halves",
        kernel,
        ids,
        (own, from_left, from_right),
        [VMEM] * 3,
        [sds(*shape), sds(*shape), sds(*own.shape)],
        after=after,
    )


def project(ids, streams, scaled, squares, pieces, weight):
    rows = scaled[0].shape[1]
    width, pair = weight.shape
    block = width // 8
    n_chunk = len(scaled)
    plan = [p[1:] for p in pieces]
    pieces = [p[0] for p in pieces]

    def kernel(ids, *refs):
        refs = list(refs)

        def take(count):
            taken = refs[:count]
            del refs[:count]
            return taken

        ys, xs, sq = take(n_chunk), take(n_chunk), take(n_chunk)
        pieces = take(len(plan))
        (mine,) = take(1)
        some, own, total, stream = take(4)
        x_buf, mine_buf, y_sem, x_sem, mine_sem = refs
        copies = [
            pltpu.make_async_copy(
                mine.at[
                    pl.ds(pl.multiple_of((i * OUTER + ids[1]) * block, block), block), :
                ],
                mine_buf.at[i],
                mine_sem.at[i],
            )
            for i in range(2)
        ]
        moves = [
            pltpu.make_async_copy(x, x_buf.at[:, :, pl.ds(start, n)], x_sem.at[t])
            for t, (x, (start, n)) in enumerate(zip(xs, CHUNKS))
        ]
        leave = [
            pltpu.make_async_copy(y, stream.at[:, pl.ds(start, n)], y_sem.at[t])
            for t, (y, (start, n)) in enumerate(zip(ys, CHUNKS))
        ]
        for c in moves + copies + leave:
            c.start()
        lanes = sq[0][...]
        for more in sq[1:]:
            lanes = lanes + more[...]
        whole_sum = jnp.sum(lanes, axis=1, keepdims=True)
        total[...] = jnp.broadcast_to(whole_sum, total.shape)
        for c in moves:
            c.wait()
        acc = [jnp.zeros((rows, pair), F32) for _ in range(3)]
        for piece, (first, count, step, crossed) in zip(pieces, plan):
            for i in range(first, first + count):
                value = x_buf[i, :, columns_of(ids, step, crossed)]
                for k in range(3):
                    there = piece[k] if count == 1 else piece[i, k]
                    acc[k] += jnp.dot(value, there, preferred_element_type=F32)
        for k in range(3):
            some[k] = acc[k]
        for c in copies:
            c.wait()
        own[...] = jnp.dot(
            x_buf[0], mine_buf[0], preferred_element_type=F32
        ) + jnp.dot(x_buf[1], mine_buf[1], preferred_element_type=F32)
        for c in leave:
            c.wait()

    return call(
        "project",
        kernel,
        ids,
        (*streams, *scaled, *squares, *pieces, weight),
        [VMEM] * (3 * n_chunk + len(plan)) + [HBM],
        [
            sds(3, rows, pair, dtype=F32),
            sds(rows, pair, dtype=F32),
            sds(rows, 128, dtype=F32),
            jax.ShapeDtypeStruct((rows, block), BF),
        ],
        [
            pltpu.VMEM((2, rows, block), BF),
            pltpu.VMEM((2, block, pair), BF),
            COPY((n_chunk,)),
            COPY((n_chunk,)),
            COPY((2,)),
        ],
        mb=8,
        out_specs=[VMEM] * 3 + [ANY],
    )


def columns_of(ids, step, crossed):
    source = lax.rem(ids[2] + 4 - step, 4)
    core = 1 - ids[3] if crossed else ids[3]
    return pl.ds(pl.multiple_of((2 * source + core) * UNIT, UNIT), UNIT)


def complete(ids, some, total, scaled, pieces):
    _, rows, pair = some.shape
    n_chunk = len(scaled)
    block = sum(n for _, n in CHUNKS)

    def kernel(ids, some, total, *refs):
        xs = refs[:n_chunk]
        a, b, *messages, x_buf = refs[n_chunk:]
        for x, (start, n) in zip(xs, CHUNKS):
            x_buf[:, :, start : start + n] = x[...]
        whole_sum = total[:, :1]
        high = whole_sum.astype(BF)
        low = (whole_sum - high.astype(F32)).astype(BF)
        lane = lax.broadcasted_iota(jnp.int32, (rows, 128), 1)
        tail = jnp.where(lane < 64, high.astype(F32), low.astype(F32)).astype(BF)
        for m in messages:
            m[:, pair:] = tail
        left = x_buf[0, :, columns_of(ids, 2, True)]
        right = x_buf[1, :, columns_of(ids, 2, True)]
        for k, m in enumerate(messages):
            value = (
                some[k]
                + jnp.dot(left, a[k], preferred_element_type=F32)
                + jnp.dot(right, b[k], preferred_element_type=F32)
            )
            m[:, :pair] = value.astype(BF)

    return call(
        "complete",
        kernel,
        ids,
        (some, total, *scaled, *pieces),
        [VMEM] * (4 + n_chunk),
        [sds(rows, pair + 128)] * 3,
        [pltpu.VMEM((2, rows, block), BF)],
    )


def finish(ids, own, total, arrived, width):
    rows, pair = own.shape

    def kernel(ids, own, total, a, b, c, out):
        value = own[...]
        squares = total[:, :1]
        for m in (a, b, c):
            value = value + m[:, :pair].astype(F32)
            tail = m[:, pair:].astype(F32)
            squares = squares + tail[:, :1] + tail[:, 64:65]
        factor = lax.rsqrt(squares * (1.0 / width) + 1e-05)
        out[...] = (value * factor).astype(BF)

    return call(
        "finish",
        kernel,
        ids,
        (own, total, *arrived),
        [VMEM] * 5,
        [jax.ShapeDtypeStruct((rows, pair), BF)],
    )[0]


def body(partials, residual, norm_gain, kv_weight):
    partial = partials[0]
    rows, width = partial.shape
    pair = kv_weight.shape[2]
    weight = kv_weight.reshape(width, pair)
    partial, weight = pin(partial, weight)
    ids = jnp.stack(
        [lax.axis_index(a).astype(jnp.int32) for a in ("inner", "outer", "x", "core")]
    )
    gain = norm_gain.reshape(width // 128, 128)

    def send(label, value, axis, pairs):
        with jax.named_scope(label):
            return lax.ppermute(value, axis, pairs)

    def cross(label, pair):
        return (
            send(label + "_a", pair[0], "outer", PAIR_A),
            send(label + "_b", pair[1], "outer", PAIR_B),
        )

    c0, c1 = CHUNKS
    *p0, own0 = pick_columns(ids, partial, c0)
    r0 = cross("first0", p0)
    *f0, keep0 = first_add(ids, own0, *r0, [COSTS[0]])
    r0 = cross("second0", f0)
    sent = pick_weights(ids, weight, [keep0])
    got = [send(f"weights{k}", s, "outer", shift(k)) for k, s in zip((1, 2, 3), sent)]
    *p1, own1 = pick_columns(ids, partial, c1, [sent[0], COSTS[2]])
    r1 = cross("first1", p1)
    local0, z0 = second_add(ids, keep0, *r0, residual, c0, [own1, COSTS[1]])
    z0 = send("inner0", z0, "inner", SWAP)
    near0 = stack(ids, got, [local0, COSTS[3]])
    near1 = send("along_x1", near0, "x", shift(1))
    near3 = send("along_x3", near0, "x", shift(3))
    *f1, keep1 = first_add(ids, own1, *r1, [near0, COSTS[4]])
    r1 = cross("second1", f1)
    local1, z1 = second_add(ids, keep1, *r1, residual, c1, [keep1, COSTS[5]])
    z1 = send("inner1", z1, "inner", SWAP)
    stream0, scaled0, squares0 = update(ids, local0, z0, gain, c0, [local1, COSTS[7]])
    left, right, across = halves(ids, near0, near1, near3, [stream0, COSTS[6]])
    near2a = send("along_x2a", left, "x", shift(1))
    near2b = send("along_x2b", right, "x", shift(3))
    stream1, scaled1, squares1 = update(ids, local1, z1, gain, c1, [left, COSTS[8]])
    far0, far1, far2a, far2b, far3 = [
        send(f"core{k}", w, "core", SWAP)
        for k, w in (("0", across), ("1", near1), ("2a", near2a), ("2b", near2b), ("3", near3))
    ]
    some, own, total, stream = project(
        ids,
        [stream0, stream1],
        [scaled0, scaled1],
        [squares0, squares1],
        [
            (near0, 0, 2, 0, False),
            (near1, 0, 2, 1, False),
            (near3, 0, 2, 3, False),
            (near2a, 0, 1, 2, False),
            (near2b, 1, 1, 2, False),
            (far0, 0, 2, 0, True),
            (far1, 0, 2, 1, True),
            (far3, 0, 2, 3, True),
        ],
        weight,
    )
    messages = complete(ids, some, total, [scaled0, scaled1], [far2a, far2b])
    arrived = [
        send(f"products{k}", m, "outer", shift(-k)) for k, m in zip((1, 2, 3), messages)
    ]
    kv = finish(ids, own, total, arrived, width)
    return stream, kv.reshape(rows, 1, pair)


def solution(mesh):
    fine = Mesh(
        mesh.devices.reshape(4, 4, 2, 2, 4), ("x", "z_lo", "core", "inner", "outer")
    )
    dp = ("x", "z_lo", "core")
    placed = (
        P((*dp, "inner", "outer"), None, None),
        P(dp, ("inner", "outer")),
        P(),
        P(None, ("inner", "outer"), None),
    )
    return jax.shard_map(
        body,
        mesh=fine,
        in_specs=placed,
        out_specs=(P(dp, ("inner", "outer")), P(dp, ("inner", "outer"), None)),
        check_vma=False,
    )
```

```python
import jax
import jax.numpy as jnp
from jax import lax
from jax.experimental import pallas as pl
from jax.experimental.pallas import tpu as pltpu
from jax.sharding import Mesh
from jax.sharding import PartitionSpec as P

BF = jnp.bfloat16
F32 = jnp.float32
OUTER = 4
UNIT = 256
CHUNKS = ((0, 1280), (1280, 768))
ANY = pl.BlockSpec(memory_space=pl.ANY)
HBM = pl.BlockSpec(memory_space=pltpu.HBM)
VMEM = pl.BlockSpec(memory_space=pltpu.VMEM)
SMEM = pl.BlockSpec(memory_space=pltpu.SMEM)
PAIR_A = [(o, o ^ 1) for o in range(4)]
PAIR_B = [(o, o ^ 3) for o in range(4)]
SWAP = [(0, 1), (1, 0)]
MB = 1024 * 1024
COSTS = (0.0, 2.0, 0.0, 2.0, 0.0, 0.0, 0.0, 4.0, 7.0)
COPY = pltpu.SemaphoreType.DMA


def shift(k):
    return [(o, (o + k) % 4) for o in range(4)]


def sds(*shape, dtype=BF):
    return pltpu.VMEM(shape, dtype)


def pin(*arrays):
    return [pltpu.with_memory_space_constraint(a, pltpu.HBM) for a in arrays]


def call(
    name, kernel, ids, args, in_specs, out_shape, scratch=(), after=(), mb=4, out_specs=None
):
    share = 0.0
    if after and isinstance(after[-1], float):
        *after, share = after
    in_specs = [SMEM, *in_specs] + [ANY] * len(after)
    args = [ids, *args, *after]
    inner = kernel
    spot = len(args) - len(after)

    def kernel(*refs):
        inner(*refs[:spot], *refs[len(args) :])

    return pl.pallas_call(
        kernel,
        in_specs=in_specs,
        out_specs=out_specs or [VMEM] * len(out_shape),
        out_shape=out_shape,
        scratch_shapes=list(scratch),
        compiler_params=pltpu.CompilerParams(vmem_limit_bytes=mb * MB),
        cost_estimate=pl.CostEstimate(
            flops=int(share * 1e9), bytes_accessed=int(share * MB), transcendentals=0
        ),
        name=name,
    )(*args)


def run(copies):
    for c in copies:
        c.start()
    for c in copies:
        c.wait()


def pick_columns(ids, partial, chunk, after=()):
    rows, width = partial.shape
    start, n = chunk
    block = width // 8

    def kernel(ids, src, to_a, to_b, own, sem):
        o = ids[1]
        run(
            [
                pltpu.make_async_copy(
                    src.at[
                        :, pl.ds(pl.multiple_of((half + there) * block + start, 128), n)
                    ],
                    out.at[slot],
                    sem.at[t],
                )
                for t, (out, slot, half, there) in enumerate(
                    (
                        (to_a, 0, 0, o ^ 1),
                        (to_a, 1, 0, o ^ 2),
                        (to_b, 0, OUTER, o ^ 3),
                        (to_b, 1, OUTER, o ^ 2),
                        (own, 0, 0, o),
                        (own, 1, 0, o ^ 3),
                        (own, 2, OUTER, o),
                        (own, 3, OUTER, o ^ 1),
                    )
                )
            ]
        )

    return call(
        "pick_columns",
        kernel,
        ids,
        (partial,),
        [HBM],
        [sds(2, rows, n), sds(2, rows, n), sds(4, rows, n)],
        [COPY((8,))],
        after,
    )


def first_add(ids, own, from_a, from_b, after=()):
    _, rows, n = own.shape

    def kernel(ids, own, ra, rb, to_a, to_b, keep):
        to_b[...] = (own[1].astype(F32) + ra[1].astype(F32)).astype(BF)
        to_a[...] = (own[3].astype(F32) + rb[1].astype(F32)).astype(BF)
        keep[0] = own[0].astype(F32) + ra[0].astype(F32)
        keep[1] = own[2].astype(F32) + rb[0].astype(F32)

    return call(
        "first_add",
        kernel,
        ids,
        (own, from_a, from_b),
        [VMEM] * 3,
        [sds(rows, n), sds(rows, n), sds(2, rows, n, dtype=F32)],
        after=after,
    )


def second_add(ids, keep, from_a, from_b, residual, chunk, after=()):
    _, rows, n = keep.shape
    start = chunk[0]

    def kernel(ids, keep, ra, rb, res, out, send):
        extra = res[:, start : start + n].astype(F32)
        zero = jnp.zeros_like(extra)
        left = keep[0] + rb[...].astype(F32) + jnp.where(ids[0] == 0, extra, zero)
        right = keep[1] + ra[...].astype(F32) + jnp.where(ids[0] == 1, extra, zero)
        out[0] = left
        out[1] = right
        send[0] = left.astype(BF)
        send[1] = right.astype(BF)

    return call(
        "second_add",
        kernel,
        ids,
        (keep, from_a, from_b, residual),
        [VMEM] * 4,
        [sds(2, rows, n, dtype=F32), sds(2, rows, n)],
        after=after,
    )


def update(ids, local, arrived, gain, chunk, after=()):
    _, rows, n = local.shape
    start = chunk[0]
    block = gain.shape[0] // 8

    def kernel(ids, local, arrived, gain, stream, scaled, squares):
        mine = ids[0] == 0
        part = jnp.zeros((rows, 128), F32)
        for u in range(n // 128):
            at = slice(u * 128, (u + 1) * 128)
            values = []
            for i in range(2):
                row = (i * OUTER + ids[1]) * block + start // 128 + u
                value = (local[i, :, at] + arrived[i, :, at].astype(F32)).astype(BF)
                wide = value.astype(F32)
                scaled[i, :, at] = (wide * gain[pl.ds(row, 1), :]).astype(BF)
                part = part + wide * wide
                values.append(wide)
            stream[:, at] = jnp.where(mine, values[0], values[1]).astype(BF)
        squares[...] = part

    return call(
        "update",
        kernel,
        ids,
        (local, arrived, gain),
        [VMEM] * 3,
        [sds(rows, n), sds(2, rows, n), sds(rows, 128, dtype=F32)],
        after=after,
    )


def pick_weights(ids, weight, after=()):
    width, pair = weight.shape
    block = width // 8

    def kernel(ids, src, *refs):
        outs, sem = refs[:3], refs[3]
        q = ids[2] * 2 + ids[3]
        copies = []
        for k in range(3):
            there = lax.rem(ids[1] + k + 1, OUTER)
            for i in range(2):
                at = pl.multiple_of((i * OUTER + there) * block + q * UNIT, UNIT)
                copies.append(
                    pltpu.make_async_copy(
                        src.at[pl.ds(at, UNIT), :], outs[k].at[i], sem.at[2 * k + i]
                    )
                )
        run(copies)

    return call(
        "pick_weights",
        kernel,
        ids,
        (weight,),
        [HBM],
        [sds(2, UNIT, pair)] * 3,
        [COPY((6,))],
        after,
    )


def stack(ids, pieces, after=()):
    shape = pieces[0].shape

    def kernel(ids, a, b, c, out):
        for k, src in enumerate((a, b, c)):
            for i in range(2):
                out[i, k] = src[i]

    return call(
        "stack",
        kernel,
        ids,
        pieces,
        [VMEM] * 3,
        [sds(2, 3, *shape[1:])],
        after=after,
    )[0]


def halves(ids, own, from_left, from_right, after=()):
    shape = from_left.shape[1:]

    def kernel(ids, own, a, b, left, right, across):
        left[...] = a[0]
        right[...] = b[1]
        across[...] = own[...]

    return call(
        "halves",
        kernel,
        ids,
        (own, from_left, from_right),
        [VMEM] * 3,
        [sds(*shape), sds(*shape), sds(*own.shape)],
        after=after,
    )


def project(ids, streams, scaled, squares, pieces, weight):
    rows = scaled[0].shape[1]
    width, pair = weight.shape
    block = width // 8
    n_chunk = len(scaled)
    plan = [p[1:] for p in pieces]
    pieces = [p[0] for p in pieces]

    def kernel(ids, *refs):
        refs = list(refs)

        def take(count):
            taken = refs[:count]
            del refs[:count]
            return taken

        ys, xs, sq = take(n_chunk), take(n_chunk), take(n_chunk)
        pieces = take(len(plan))
        (mine,) = take(1)
        some, own, total, stream = take(4)
        x_buf, mine_buf, y_sem, x_sem, mine_sem = refs
        copies = [
            pltpu.make_async_copy(
                mine.at[
                    pl.ds(pl.multiple_of((i * OUTER + ids[1]) * block, block), block), :
                ],
                mine_buf.at[i],
                mine_sem.at[i],
            )
            for i in range(2)
        ]
        moves = [
            pltpu.make_async_copy(x, x_buf.at[:, :, pl.ds(start, n)], x_sem.at[t])
            for t, (x, (start, n)) in enumerate(zip(xs, CHUNKS))
        ]
        leave = [
            pltpu.make_async_copy(y, stream.at[:, pl.ds(start, n)], y_sem.at[t])
            for t, (y, (start, n)) in enumerate(zip(ys, CHUNKS))
        ]
        for c in moves + copies + leave:
            c.start()
        lanes = sq[0][...]
        for more in sq[1:]:
            lanes = lanes + more[...]
        whole_sum = jnp.sum(lanes, axis=1, keepdims=True)
        total[...] = jnp.broadcast_to(whole_sum, total.shape)
        for c in moves:
            c.wait()
        acc = [jnp.zeros((rows, pair), F32) for _ in range(3)]
        for piece, (first, count, step, crossed) in zip(pieces, plan):
            for i in range(first, first + count):
                value = x_buf[i, :, columns_of(ids, step, crossed)]
                for k in range(3):
                    there = piece[k] if count == 1 else piece[i, k]
                    acc[k] += jnp.dot(value, there, preferred_element_type=F32)
        for k in range(3):
            some[k] = acc[k]
        for c in copies:
            c.wait()
        own[...] = jnp.dot(
            x_buf[0], mine_buf[0], preferred_element_type=F32
        ) + jnp.dot(x_buf[1], mine_buf[1], preferred_element_type=F32)
        for c in leave:
            c.wait()

    return call(
        "project",
        kernel,
        ids,
        (*streams, *scaled, *squares, *pieces, weight),
        [VMEM] * (3 * n_chunk + len(plan)) + [HBM],
        [
            sds(3, rows, pair, dtype=F32),
            sds(rows, pair, dtype=F32),
            sds(rows, 128, dtype=F32),
            jax.ShapeDtypeStruct((rows, block), BF),
        ],
        [
            pltpu.VMEM((2, rows, block), BF),
            pltpu.VMEM((2, block, pair), BF),
            COPY((n_chunk,)),
            COPY((n_chunk,)),
            COPY((2,)),
        ],
        mb=8,
        out_specs=[VMEM] * 3 + [ANY],
    )


def columns_of(ids, step, crossed):
    source = lax.rem(ids[2] + 4 - step, 4)
    core = 1 - ids[3] if crossed else ids[3]
    return pl.ds(pl.multiple_of((2 * source + core) * UNIT, UNIT), UNIT)


def complete(ids, some, total, scaled, pieces):
    _, rows, pair = some.shape
    n_chunk = len(scaled)
    block = sum(n for _, n in CHUNKS)

    def kernel(ids, some, total, *refs):
        xs = refs[:n_chunk]
        a, b, *messages, x_buf = refs[n_chunk:]
        for x, (start, n) in zip(xs, CHUNKS):
            x_buf[:, :, start : start + n] = x[...]
        whole_sum = total[:, :1]
        high = whole_sum.astype(BF)
        low = (whole_sum - high.astype(F32)).astype(BF)
        lane = lax.broadcasted_iota(jnp.int32, (rows, 128), 1)
        tail = jnp.where(lane < 64, high.astype(F32), low.astype(F32)).astype(BF)
        for m in messages:
            m[:, pair:] = tail
        left = x_buf[0, :, columns_of(ids, 2, True)]
        right = x_buf[1, :, columns_of(ids, 2, True)]
        for k, m in enumerate(messages):
            value = (
                some[k]
                + jnp.dot(left, a[k], preferred_element_type=F32)
                + jnp.dot(right, b[k], preferred_element_type=F32)
            )
            m[:, :pair] = value.astype(BF)

    return call(
        "complete",
        kernel,
        ids,
        (some, total, *scaled, *pieces),
        [VMEM] * (4 + n_chunk),
        [sds(rows, pair + 128)] * 3,
        [pltpu.VMEM((2, rows, block), BF)],
    )


def finish(ids, own, total, arrived, width):
    rows, pair = own.shape

    def kernel(ids, own, total, a, b, c, out):
        value = own[...]
        squares = total[:, :1]
        for m in (a, b, c):
            value = value + m[:, :pair].astype(F32)
            tail = m[:, pair:].astype(F32)
            squares = squares + tail[:, :1] + tail[:, 64:65]
        factor = lax.rsqrt(squares * (1.0 / width) + 1e-05)
        out[...] = (value * factor).astype(BF)

    return call(
        "finish",
        kernel,
        ids,
        (own, total, *arrived),
        [VMEM] * 5,
        [jax.ShapeDtypeStruct((rows, pair), BF)],
    )[0]


def body(partials, residual, norm_gain, kv_weight):
    partial = partials[0]
    rows, width = partial.shape
    pair = kv_weight.shape[2]
    weight = kv_weight.reshape(width, pair)
    partial, weight = pin(partial, weight)
    ids = jnp.stack(
        [lax.axis_index(a).astype(jnp.int32) for a in ("inner", "outer", "x", "core")]
    )
    gain = norm_gain.reshape(width // 128, 128)

    def send(label, value, axis, pairs):
        with jax.named_scope(label):
            return lax.ppermute(value, axis, pairs)

    def cross(label, pair):
        return (
            send(label + "_a", pair[0], "outer", PAIR_A),
            send(label + "_b", pair[1], "outer", PAIR_B),
        )

    c0, c1 = CHUNKS
    *p0, own0 = pick_columns(ids, partial, c0)
    r0 = cross("first0", p0)
    *f0, keep0 = first_add(ids, own0, *r0, [COSTS[0]])
    r0 = cross("second0", f0)
    sent = pick_weights(ids, weight, [keep0])
    got = [send(f"weights{k}", s, "outer", shift(k)) for k, s in zip((1, 2, 3), sent)]
    *p1, own1 = pick_columns(ids, partial, c1, [sent[0], COSTS[2]])
    r1 = cross("first1", p1)
    local0, z0 = second_add(ids, keep0, *r0, residual, c0, [own1, COSTS[1]])
    z0 = send("inner0", z0, "inner", SWAP)
    near0 = stack(ids, got, [local0, COSTS[3]])
    near1 = send("along_x1", near0, "x", shift(1))
    near3 = send("along_x3", near0, "x", shift(3))
    *f1, keep1 = first_add(ids, own1, *r1, [near0, COSTS[4]])
    r1 = cross("second1", f1)
    local1, z1 = second_add(ids, keep1, *r1, residual, c1, [keep1, COSTS[5]])
    z1 = send("inner1", z1, "inner", SWAP)
    stream0, scaled0, squares0 = update(ids, local0, z0, gain, c0, [local1, COSTS[7]])
    left, right, across = halves(ids, near0, near1, near3, [stream0, COSTS[6]])
    near2a = send("along_x2a", left, "x", shift(1))
    near2b = send("along_x2b", right, "x", shift(3))
    stream1, scaled1, squares1 = update(ids, local1, z1, gain, c1, [left, COSTS[8]])
    far0, far1, far2a, far2b, far3 = [
        send(f"core{k}", w, "core", SWAP)
        for k, w in (("0", across), ("1", near1), ("2a", near2a), ("2b", near2b), ("3", near3))
    ]
    some, own, total, stream = project(
        ids,
        [stream0, stream1],
        [scaled0, scaled1],
        [squares0, squares1],
        [
            (near0, 0, 2, 0, False),
            (near1, 0, 2, 1, False),
            (near3, 0, 2, 3, False),
            (near2a, 0, 1, 2, False),
            (near2b, 1, 1, 2, False),
            (far0, 0, 2, 0, True),
            (far1, 0, 2, 1, True),
            (far3, 0, 2, 3, True),
        ],
        weight,
    )
    messages = complete(ids, some, total, [scaled0, scaled1], [far2a, far2b])
    arrived = [
        send(f"products{k}", m, "outer", shift(-k)) for k, m in zip((1, 2, 3), messages)
    ]
    kv = finish(ids, own, total, arrived, width)
    return stream, kv.reshape(rows, 1, pair)


def solution(mesh):
    fine = Mesh(
        mesh.devices.reshape(4, 4, 2, 2, 4), ("x", "z_lo", "core", "inner", "outer")
    )
    dp = ("x", "z_lo", "core")
    placed = (
        P((*dp, "inner", "outer"), None, None),
        P(dp, ("inner", "outer")),
        P(),
        P(None, ("inner", "outer"), None),
    )
    return jax.shard_map(
        body,
        mesh=fine,
        in_specs=placed,
        out_specs=(P(dp, ("inner", "outer")), P(dp, ("inner", "outer"), None)),
        check_vma=False,
    )
```

```python
import jax
import jax.numpy as jnp
from jax import lax
from jax.experimental import pallas as pl
from jax.experimental.pallas import tpu as pltpu
from jax.sharding import Mesh
from jax.sharding import PartitionSpec as P

BF = jnp.bfloat16
F32 = jnp.float32
OUTER = 4
UNIT = 256
CHUNKS = ((0, 1152), (1152, 896))
ANY = pl.BlockSpec(memory_space=pl.ANY)
HBM = pl.BlockSpec(memory_space=pltpu.HBM)
VMEM = pl.BlockSpec(memory_space=pltpu.VMEM)
SMEM = pl.BlockSpec(memory_space=pltpu.SMEM)
PAIR_A = [(o, o ^ 1) for o in range(4)]
PAIR_B = [(o, o ^ 3) for o in range(4)]
SWAP = [(0, 1), (1, 0)]
MB = 1024 * 1024
COSTS = (0.0, 4.0, 0.0, 12.0, 0.0, 0.0, 0.0, 4.0, 10.0)
COPY = pltpu.SemaphoreType.DMA


def shift(k):
    return [(o, (o + k) % 4) for o in range(4)]


def sds(*shape, dtype=BF):
    return pltpu.VMEM(shape, dtype)


def pin(*arrays):
    return [pltpu.with_memory_space_constraint(a, pltpu.HBM) for a in arrays]


def call(
    name, kernel, ids, args, in_specs, out_shape, scratch=(), after=(), mb=4, out_specs=None
):
    share = 0.0
    if after and isinstance(after[-1], float):
        *after, share = after
    in_specs = [SMEM, *in_specs] + [ANY] * len(after)
    args = [ids, *args, *after]
    inner = kernel
    spot = len(args) - len(after)

    def kernel(*refs):
        inner(*refs[:spot], *refs[len(args) :])

    return pl.pallas_call(
        kernel,
        in_specs=in_specs,
        out_specs=out_specs or [VMEM] * len(out_shape),
        out_shape=out_shape,
        scratch_shapes=list(scratch),
        compiler_params=pltpu.CompilerParams(vmem_limit_bytes=mb * MB),
        cost_estimate=pl.CostEstimate(
            flops=int(share * 1e9), bytes_accessed=int(share * MB), transcendentals=0
        ),
        name=name,
    )(*args)


def run(copies):
    for c in copies:
        c.start()
    for c in copies:
        c.wait()


def pick_columns(ids, partial, chunk, after=()):
    rows, width = partial.shape
    start, n = chunk
    block = width // 8

    def kernel(ids, src, to_a, to_b, own, sem):
        o = ids[1]
        run(
            [
                pltpu.make_async_copy(
                    src.at[
                        :, pl.ds(pl.multiple_of((half + there) * block + start, 128), n)
                    ],
                    out.at[slot],
                    sem.at[t],
                )
                for t, (out, slot, half, there) in enumerate(
                    (
                        (to_a, 0, 0, o ^ 1),
                        (to_a, 1, 0, o ^ 2),
                        (to_b, 0, OUTER, o ^ 3),
                        (to_b, 1, OUTER, o ^ 2),
                        (own, 0, 0, o),
                        (own, 1, 0, o ^ 3),
                        (own, 2, OUTER, o),
                        (own, 3, OUTER, o ^ 1),
                    )
                )
            ]
        )

    return call(
        "pick_columns",
        kernel,
        ids,
        (partial,),
        [HBM],
        [sds(2, rows, n), sds(2, rows, n), sds(4, rows, n)],
        [COPY((8,))],
        after,
    )


def first_add(ids, own, from_a, from_b, after=()):
    _, rows, n = own.shape

    def kernel(ids, own, ra, rb, to_a, to_b, keep):
        to_b[...] = (own[1].astype(F32) + ra[1].astype(F32)).astype(BF)
        to_a[...] = (own[3].astype(F32) + rb[1].astype(F32)).astype(BF)
        keep[0] = own[0].astype(F32) + ra[0].astype(F32)
        keep[1] = own[2].astype(F32) + rb[0].astype(F32)

    return call(
        "first_add",
        kernel,
        ids,
        (own, from_a, from_b),
        [VMEM] * 3,
        [sds(rows, n), sds(rows, n), sds(2, rows, n, dtype=F32)],
        after=after,
    )


def second_add(ids, keep, from_a, from_b, residual, chunk, after=()):
    _, rows, n = keep.shape
    start = chunk[0]

    def kernel(ids, keep, ra, rb, res, out, send):
        extra = res[:, start : start + n].astype(F32)
        zero = jnp.zeros_like(extra)
        left = keep[0] + rb[...].astype(F32) + jnp.where(ids[0] == 0, extra, zero)
        right = keep[1] + ra[...].astype(F32) + jnp.where(ids[0] == 1, extra, zero)
        out[0] = left
        out[1] = right
        send[0] = left.astype(BF)
        send[1] = right.astype(BF)

    return call(
        "second_add",
        kernel,
        ids,
        (keep, from_a, from_b, residual),
        [VMEM] * 4,
        [sds(2, rows, n, dtype=F32), sds(2, rows, n)],
        after=after,
    )


def update(ids, local, arrived, gain, chunk, after=()):
    _, rows, n = local.shape
    start = chunk[0]
    block = gain.shape[0] // 8

    def kernel(ids, local, arrived, gain, stream, scaled, squares):
        mine = ids[0] == 0
        part = jnp.zeros((rows, 128), F32)
        for u in range(n // 128):
            at = slice(u * 128, (u + 1) * 128)
            values = []
            for i in range(2):
                row = (i * OUTER + ids[1]) * block + start // 128 + u
                value = (local[i, :, at] + arrived[i, :, at].astype(F32)).astype(BF)
                wide = value.astype(F32)
                scaled[i, :, at] = (wide * gain[pl.ds(row, 1), :]).astype(BF)
                part = part + wide * wide
                values.append(wide)
            stream[:, at] = jnp.where(mine, values[0], values[1]).astype(BF)
        squares[...] = part

    return call(
        "update",
        kernel,
        ids,
        (local, arrived, gain),
        [VMEM] * 3,
        [sds(rows, n), sds(2, rows, n), sds(rows, 128, dtype=F32)],
        after=after,
    )


def pick_weights(ids, weight, after=()):
    width, pair = weight.shape
    block = width // 8

    def kernel(ids, src, *refs):
        outs, sem = refs[:3], refs[3]
        q = ids[2] * 2 + ids[3]
        copies = []
        for k in range(3):
            there = lax.rem(ids[1] + k + 1, OUTER)
            for i in range(2):
                at = pl.multiple_of((i * OUTER + there) * block + q * UNIT, UNIT)
                copies.append(
                    pltpu.make_async_copy(
                        src.at[pl.ds(at, UNIT), :], outs[k].at[i], sem.at[2 * k + i]
                    )
                )
        run(copies)

    return call(
        "pick_weights",
        kernel,
        ids,
        (weight,),
        [HBM],
        [sds(2, UNIT, pair)] * 3,
        [COPY((6,))],
        after,
    )


def stack(ids, pieces, after=()):
    shape = pieces[0].shape

    def kernel(ids, a, b, c, out):
        for k, src in enumerate((a, b, c)):
            for i in range(2):
                out[i, k] = src[i]

    return call(
        "stack",
        kernel,
        ids,
        pieces,
        [VMEM] * 3,
        [sds(2, 3, *shape[1:])],
        after=after,
    )[0]


def halves(ids, own, from_left, from_right, after=()):
    shape = from_left.shape[1:]

    def kernel(ids, own, a, b, left, right, across):
        left[...] = a[0]
        right[...] = b[1]
        across[...] = own[...]

    return call(
        "halves",
        kernel,
        ids,
        (own, from_left, from_right),
        [VMEM] * 3,
        [sds(*shape), sds(*shape), sds(*own.shape)],
        after=after,
    )


def project(ids, streams, scaled, squares, pieces, weight):
    rows = scaled[0].shape[1]
    width, pair = weight.shape
    block = width // 8
    n_chunk = len(scaled)
    plan = [p[1:] for p in pieces]
    pieces = [p[0] for p in pieces]

    def kernel(ids, *refs):
        refs = list(refs)

        def take(count):
            taken = refs[:count]
            del refs[:count]
            return taken

        ys, xs, sq = take(n_chunk), take(n_chunk), take(n_chunk)
        pieces = take(len(plan))
        (mine,) = take(1)
        some, own, total, stream = take(4)
        x_buf, mine_buf, y_sem, x_sem, mine_sem = refs
        copies = [
            pltpu.make_async_copy(
                mine.at[
                    pl.ds(pl.multiple_of((i * OUTER + ids[1]) * block, block), block), :
                ],
                mine_buf.at[i],
                mine_sem.at[i],
            )
            for i in range(2)
        ]
        moves = [
            pltpu.make_async_copy(x, x_buf.at[:, :, pl.ds(start, n)], x_sem.at[t])
            for t, (x, (start, n)) in enumerate(zip(xs, CHUNKS))
        ]
        leave = [
            pltpu.make_async_copy(y, stream.at[:, pl.ds(start, n)], y_sem.at[t])
            for t, (y, (start, n)) in enumerate(zip(ys, CHUNKS))
        ]
        for c in moves + copies + leave:
            c.start()
        lanes = sq[0][...]
        for more in sq[1:]:
            lanes = lanes + more[...]
        whole_sum = jnp.sum(lanes, axis=1, keepdims=True)
        total[...] = jnp.broadcast_to(whole_sum, total.shape)
        for c in moves:
            c.wait()
        acc = [jnp.zeros((rows, pair), F32) for _ in range(3)]
        for piece, (first, count, step, crossed) in zip(pieces, plan):
            for i in range(first, first + count):
                value = x_buf[i, :, columns_of(ids, step, crossed)]
                for k in range(3):
                    there = piece[k] if count == 1 else piece[i, k]
                    acc[k] += jnp.dot(value, there, preferred_element_type=F32)
        for k in range(3):
            some[k] = acc[k]
        for c in copies:
            c.wait()
        own[...] = jnp.dot(
            x_buf[0], mine_buf[0], preferred_element_type=F32
        ) + jnp.dot(x_buf[1], mine_buf[1], preferred_element_type=F32)
        for c in leave:
            c.wait()

    return call(
        "project",
        kernel,
        ids,
        (*streams, *scaled, *squares, *pieces, weight),
        [VMEM] * (3 * n_chunk + len(plan)) + [HBM],
        [
            sds(3, rows, pair, dtype=F32),
            sds(rows, pair, dtype=F32),
            sds(rows, 128, dtype=F32),
            jax.ShapeDtypeStruct((rows, block), BF),
        ],
        [
            pltpu.VMEM((2, rows, block), BF),
            pltpu.VMEM((2, block, pair), BF),
            COPY((n_chunk,)),
            COPY((n_chunk,)),
            COPY((2,)),
        ],
        mb=8,
        out_specs=[VMEM] * 3 + [ANY],
    )


def columns_of(ids, step, crossed):
    source = lax.rem(ids[2] + 4 - step, 4)
    core = 1 - ids[3] if crossed else ids[3]
    return pl.ds(pl.multiple_of((2 * source + core) * UNIT, UNIT), UNIT)


def complete(ids, some, total, scaled, pieces):
    _, rows, pair = some.shape
    n_chunk = len(scaled)
    block = sum(n for _, n in CHUNKS)

    def kernel(ids, some, total, *refs):
        xs = refs[:n_chunk]
        a, b, *messages, x_buf = refs[n_chunk:]
        for x, (start, n) in zip(xs, CHUNKS):
            x_buf[:, :, start : start + n] = x[...]
        whole_sum = total[:, :1]
        high = whole_sum.astype(BF)
        low = (whole_sum - high.astype(F32)).astype(BF)
        lane = lax.broadcasted_iota(jnp.int32, (rows, 128), 1)
        tail = jnp.where(lane < 64, high.astype(F32), low.astype(F32)).astype(BF)
        for m in messages:
            m[:, pair:] = tail
        left = x_buf[0, :, columns_of(ids, 2, True)]
        right = x_buf[1, :, columns_of(ids, 2, True)]
        for k, m in enumerate(messages):
            value = (
                some[k]
                + jnp.dot(left, a[k], preferred_element_type=F32)
                + jnp.dot(right, b[k], preferred_element_type=F32)
            )
            m[:, :pair] = value.astype(BF)

    return call(
        "complete",
        kernel,
        ids,
        (some, total, *scaled, *pieces),
        [VMEM] * (4 + n_chunk),
        [sds(rows, pair + 128)] * 3,
        [pltpu.VMEM((2, rows, block), BF)],
    )


def finish(ids, own, total, arrived, width):
    rows, pair = own.shape

    def kernel(ids, own, total, a, b, c, out):
        value = own[...]
        squares = total[:, :1]
        for m in (a, b, c):
            value = value + m[:, :pair].astype(F32)
            tail = m[:, pair:].astype(F32)
            squares = squares + tail[:, :1] + tail[:, 64:65]
        factor = lax.rsqrt(squares * (1.0 / width) + 1e-05)
        out[...] = (value * factor).astype(BF)

    return call(
        "finish",
        kernel,
        ids,
        (own, total, *arrived),
        [VMEM] * 5,
        [jax.ShapeDtypeStruct((rows, pair), BF)],
    )[0]


def body(partials, residual, norm_gain, kv_weight):
    partial = partials[0]
    rows, width = partial.shape
    pair = kv_weight.shape[2]
    weight = kv_weight.reshape(width, pair)
    partial, weight = pin(partial, weight)
    ids = jnp.stack(
        [lax.axis_index(a).astype(jnp.int32) for a in ("inner", "outer", "x", "core")]
    )
    gain = norm_gain.reshape(width // 128, 128)

    def send(label, value, axis, pairs):
        with jax.named_scope(label):
            return lax.ppermute(value, axis, pairs)

    def cross(label, pair):
        return (
            send(label + "_a", pair[0], "outer", PAIR_A),
            send(label + "_b", pair[1], "outer", PAIR_B),
        )

    c0, c1 = CHUNKS
    *p0, own0 = pick_columns(ids, partial, c0)
    r0 = cross("first0", p0)
    *f0, keep0 = first_add(ids, own0, *r0, [COSTS[0]])
    r0 = cross("second0", f0)
    sent = pick_weights(ids, weight, [keep0])
    got = [send(f"weights{k}", s, "outer", shift(k)) for k, s in zip((1, 2, 3), sent)]
    *p1, own1 = pick_columns(ids, partial, c1, [sent[0], COSTS[2]])
    r1 = cross("first1", p1)
    local0, z0 = second_add(ids, keep0, *r0, residual, c0, [own1, COSTS[1]])
    z0 = send("inner0", z0, "inner", SWAP)
    near0 = stack(ids, got, [local0, COSTS[3]])
    near1 = send("along_x1", near0, "x", shift(1))
    near3 = send("along_x3", near0, "x", shift(3))
    *f1, keep1 = first_add(ids, own1, *r1, [near0, COSTS[4]])
    r1 = cross("second1", f1)
    local1, z1 = second_add(ids, keep1, *r1, residual, c1, [keep1, COSTS[5]])
    z1 = send("inner1", z1, "inner", SWAP)
    stream0, scaled0, squares0 = update(ids, local0, z0, gain, c0, [local1, COSTS[7]])
    left, right, across = halves(ids, near0, near1, near3, [stream0, COSTS[6]])
    near2a = send("along_x2a", left, "x", shift(1))
    near2b = send("along_x2b", right, "x", shift(3))
    stream1, scaled1, squares1 = update(ids, local1, z1, gain, c1, [left, COSTS[8]])
    far0, far1, far2a, far2b, far3 = [
        send(f"core{k}", w, "core", SWAP)
        for k, w in (("0", across), ("1", near1), ("2a", near2a), ("2b", near2b), ("3", near3))
    ]
    some, own, total, stream = project(
        ids,
        [stream0, stream1],
        [scaled0, scaled1],
        [squares0, squares1],
        [
            (near0, 0, 2, 0, False),
            (near1, 0, 2, 1, False),
            (near3, 0, 2, 3, False),
            (near2a, 0, 1, 2, False),
            (near2b, 1, 1, 2, False),
            (far0, 0, 2, 0, True),
            (far1, 0, 2, 1, True),
            (far3, 0, 2, 3, True),
        ],
        weight,
    )
    messages = complete(ids, some, total, [scaled0, scaled1], [far2a, far2b])
    arrived = [
        send(f"products{k}", m, "outer", shift(-k)) for k, m in zip((1, 2, 3), messages)
    ]
    kv = finish(ids, own, total, arrived, width)
    return stream, kv.reshape(rows, 1, pair)


def solution(mesh):
    fine = Mesh(
        mesh.devices.reshape(4, 4, 2, 2, 4), ("x", "z_lo", "core", "inner", "outer")
    )
    dp = ("x", "z_lo", "core")
    placed = (
        P((*dp, "inner", "outer"), None, None),
        P(dp, ("inner", "outer")),
        P(),
        P(None, ("inner", "outer"), None),
    )
    return jax.shard_map(
        body,
        mesh=fine,
        in_specs=placed,
        out_specs=(P(dp, ("inner", "outer")), P(dp, ("inner", "outer"), None)),
        check_vma=False,
    )
```
